256 devices in a mesh: ctx: 64 (over x_lo, y, z), head: 4 (over x_hi, core).
Axes of the slice: x: 4 (x_hi: 2, x_lo: 2; x = x_hi * 2 + x_lo), y: 4, z: 8, core: 2. Of those that a mesh axis runs over, the one named last changes fastest.
Arguments:
- queries: bfloat16 [8192, 2048], P('ctx', 'head')
- keys: bfloat16 [8192, 1024], P('ctx', 'head')
- values: bfloat16 [8192, 1024], P('ctx', 'head'), may hold values from -6 to 6
- positions: int32 [8192], P('ctx'), may hold values from 0 to 12287, as said below
- query_gain: float32 [128], replicated, as said below
- key_gain: float32 [128], replicated, as said below
- out_weight: bfloat16 [2048, 5376], P('head'), may hold values from -0.125 to 0.125
Outputs:
- mixed_rows: bfloat16 [8192, 5376], P(('ctx', 'head'))
The draws below stay inside these ranges and needn't reach their ends.
Inputs may be any that keep to these rules, and one draw needn't show every extreme that they name: `positions`: rise strictly along the document by 1 or 2 a token; the first is 0 and the last is 12287. `query_gain`: positive. `key_gain`: positive.
All inputs are finite; a program needn't handle non-finite values.
Results may differ from the reference program's by a relative error of at most 0.015.
Values may be sent and summed in bfloat16 or wider, within the bound.
No kernel may reach another device: no remote copies, remote signals or barrier semaphores. Data moves between devices by JAX's collectives and lax.ppermute only.
A program may use at most 128 MiB of HBM per device.

```python
import math
import jax
import jax.numpy as jnp
import numpy as np
from jax import lax

D = 5376
HD = 128
QH = 16
KVH = 8
BLOCK = 64
TOKENS = 8192
N_CTX = 64


def draw_keys(key, part):
    key = jax.random.fold_in(key, 1)
    result = jax.random.truncated_normal(key, -6.0, 6.0, (TOKENS, KVH, HD), jnp.float32)
    return result.reshape(TOKENS, KVH * HD).astype(jnp.bfloat16)


def draw_queries(key, part):
    key = jax.random.fold_in(key, 2)
    result = jax.random.truncated_normal(key, -6.0, 6.0, (TOKENS, QH, HD), jnp.float32)
    return result.reshape(TOKENS, QH * HD).astype(jnp.bfloat16)


def draw_query_gain(key, part):
    key = jax.random.fold_in(key, 3)
    logs = jax.random.uniform(key, (HD,), jnp.float32, jnp.log(0.8), jnp.log(2.5))
    return jnp.exp(logs)


def draw_key_gain(key, part):
    key = jax.random.fold_in(key, 4)
    logs = jax.random.uniform(key, (HD,), jnp.float32, jnp.log(0.8), jnp.log(2.5))
    return jnp.exp(logs)


def draw_positions(key, part):
    key = jax.random.fold_in(key, 6)
    shuffled = jax.random.permutation(key, TOKENS - 1)
    stride = jnp.where(shuffled < TOKENS // 2, 2, 1).astype(jnp.int32)
    return jnp.concatenate([jnp.zeros((1,), jnp.int32), jnp.cumsum(stride).astype(jnp.int32)])


def block_scale(rng, shape, pieces, least, high):
    gain = 1.0
    for dim, blocks in pieces:
        steps = jax.random.uniform(jax.random.fold_in(jax.random.fold_in(rng, 6), dim), (blocks,), jnp.float32, least / len(pieces), high / len(pieces))
        gain = gain * jnp.repeat(jnp.exp(steps), shape[dim] // blocks).reshape((-1,) + (1,) * (len(shape) - 1 - dim))
    return gain


def normal_values(stream_key, shape, scale, most, split=(), held_as=jnp.bfloat16):
    values = jax.random.normal(stream_key, shape, jnp.float32) * scale
    if len(split) > 0:
        values = block_scale(stream_key, shape, split, -0.22, 0.18) * values
    return jnp.clip(values, min=-most, max=most).astype(held_as)


def setup_inputs(seed: int = 0) -> dict:
    arg_keys = jax.random.split(jax.random.key(seed), 8)
    return {
        "queries": draw_queries(jax.random.fold_in(arg_keys[7], 71), 0),
        "keys": draw_keys(jax.random.fold_in(arg_keys[7], 71), 0),
        "values": normal_values(arg_keys[2], (TOKENS, KVH * HD), 1.0, 6.0, ((0, 64), (1, 4))),
        "positions": draw_positions(jax.random.fold_in(arg_keys[7], 71), 0),
        "query_gain": draw_query_gain(jax.random.fold_in(arg_keys[7], 71), 0),
        "key_gain": draw_key_gain(jax.random.fold_in(arg_keys[7], 71), 0),
        "out_weight": normal_values(arg_keys[6], (QH * HD, D), (QH * HD) ** -0.5, 0.125, ((0, 4),)),
    }


ROPE_BASE = 1000000.0
EPSILON = 1e-06
SCALE = 168.0 ** (-0.5)
NEGATIVE = -1e+30

def normed(vectors, scaling):
    return vectors * lax.rsqrt(lax.optimization_barrier(jnp.mean(vectors * vectors, axis=-1, keepdims=True)) + EPSILON) * scaling

def rotated(vectors, token_positions):
    half_width = vectors.shape[-1] // 2
    frequency = ROPE_BASE ** (-2.0 * jnp.arange(half_width, dtype=jnp.float32) / vectors.shape[-1])
    angles = token_positions.astype(jnp.float32)[:, None] * frequency[None, :]
    cosines = jnp.cos(angles)[:, None, :]
    sines = jnp.sin(angles)[:, None, :]
    leading = vectors[..., :half_width]
    trailing = vectors[..., half_width:]
    return jnp.concatenate([leading * cosines - trailing * sines, trailing * cosines + leading * sines], axis=-1)

def prepare(vectors, token_positions, scaling, head_width):
    row_total = vectors.shape[0]
    shaped = vectors.astype(jnp.float32).reshape(row_total, -1, head_width)
    return rotated(normed(shaped, scaling), token_positions).astype(jnp.bfloat16).reshape(row_total, -1)

def reference(queries, keys, values, positions, query_gain, key_gain, out_weight):
    head_width = query_gain.shape[0]
    total_rows = queries.shape[0]
    groups = QH // KVH
    query_rows = lax.optimization_barrier(prepare(queries, positions, query_gain, head_width))
    key_rows = lax.optimization_barrier(prepare(keys, positions, key_gain, head_width))
    key_rows = key_rows.astype(jnp.float32).reshape(total_rows, KVH, head_width)
    value_rows = values.astype(jnp.float32).reshape(total_rows, KVH, head_width)
    step_rows = math.gcd(total_rows, 256)
    key_marks = jnp.arange(total_rows, dtype=jnp.int32)

    def one_block(first_row):
        query_block = lax.dynamic_slice_in_dim(query_rows, first_row, step_rows, 0)
        query_block = query_block.astype(jnp.float32).reshape(step_rows, KVH, groups, head_width)
        scores = jnp.einsum('qgrd,kgd->grqk', query_block, key_rows) * SCALE
        query_marks = first_row + jnp.arange(step_rows, dtype=jnp.int32)
        visible = key_marks[None, :] <= query_marks[:, None]
        scores = jnp.where(visible, scores, NEGATIVE)
        highest = lax.optimization_barrier(jnp.max(scores, axis=-1, keepdims=True))
        weights = jnp.where(visible, jnp.exp(scores - highest), 0.0)
        totals = lax.optimization_barrier(jnp.sum(weights, axis=-1))
        rounded = lax.optimization_barrier(weights.astype(jnp.bfloat16)).astype(jnp.float32)
        summed = jnp.einsum('grqk,kgd->grqd', rounded, value_rows)
        normal = summed / totals[..., None]
        return jnp.transpose(normal, (2, 0, 1, 3)).reshape(step_rows, QH * head_width).astype(jnp.bfloat16)
    starts = jnp.arange(total_rows // step_rows, dtype=jnp.int32) * step_rows
    attended = lax.map(one_block, starts).reshape(total_rows, QH * head_width)
    mixed_rows = jnp.dot(attended, out_weight, preferred_element_type=jnp.float32).astype(jnp.bfloat16)
    fold_order = np.stack([np.arange(N_CTX), 2 * N_CTX - 1 - np.arange(N_CTX)], axis=1).reshape(-1)
    return mixed_rows.reshape(2 * N_CTX, BLOCK, -1)[fold_order].reshape(total_rows, -1)
```

```python
import functools

import jax
import jax.numpy as jnp
import numpy as np
from jax import lax
from jax.experimental import pallas as pl
from jax.experimental.pallas import tpu as pltpu
from jax.sharding import Mesh
from jax.sharding import PartitionSpec as P

EPSILON = 1e-06
HD = 128
PIECE = 128
NX, NY, NZ = 2, 4, 8
GROUP = NX * NY
QUERY_FACTOR = float(168.0**-0.5 / np.log(2.0))
NEGATIVE = -1e30
FREQUENCY = (1000000.0 ** (-2.0 * np.arange(64, dtype=np.float64) / 128)).astype(np.float32)
VMEM_LIMIT = 48 * 1024 * 1024
NT = (((1,), (1,)), ((), ()))


def pairs(count, partner):
    return [(i, partner(i)) for i in range(count)]


Z_PAIRS = (pairs(NZ, lambda i: i ^ 1), pairs(NZ, lambda i: (((i + 1) ^ 1) + 7) % 8))
Y_PAIRS = (pairs(NY, lambda i: i ^ 1), pairs(NY, lambda i: i ^ 3))
X_PAIRS = pairs(NX, lambda i: i ^ 1)


def prepare_kernel(q_ref, k_ref, pos_ref, freq_ref, qg_ref, kg_ref, q_out, k_out):
    lane = lax.broadcasted_iota(jnp.int32, (PIECE, HD), 1)
    angles = pos_ref[...].astype(jnp.float32) * freq_ref[...]
    cosines = jnp.cos(angles)
    sines = jnp.where(lane < HD // 2, -1.0, 1.0) * jnp.sin(angles)

    def rotate(vector, gain):
        vector = vector.astype(jnp.float32)
        normed = vector * lax.rsqrt(jnp.mean(vector * vector, axis=-1, keepdims=True) + EPSILON) * gain
        return normed * cosines + pltpu.roll(normed, HD // 2, 1) * sines

    for head in range(4):
        cols = slice(head * HD, (head + 1) * HD)
        q_out[:, cols] = (rotate(q_ref[:, cols], qg_ref[...]) * QUERY_FACTOR).astype(jnp.bfloat16)
    for head in range(2):
        cols = slice(head * HD, (head + 1) * HD)
        k_out[:, cols] = rotate(k_ref[:, cols], kg_ref[...]).astype(jnp.bfloat16)


def prepare(queries, keys, positions, query_gain, key_gain):
    freq = jnp.asarray(np.concatenate([FREQUENCY, FREQUENCY])[None, :])
    return pl.pallas_call(
        prepare_kernel,
        out_shape=(
            jax.ShapeDtypeStruct(queries.shape, jnp.bfloat16),
            jax.ShapeDtypeStruct(keys.shape, jnp.bfloat16),
        ),
    )(queries, keys, positions[:, None], freq, query_gain[None, :], key_gain[None, :])


def gather_z(own, first):
    here, there = Z_PAIRS[first], Z_PAIRS[1 - first]
    one = lax.ppermute(own, "z", here)
    two = lax.ppermute(jnp.concatenate([own, one], axis=0), "z", there)
    three = lax.ppermute(two, "z", here)
    four = lax.ppermute(three, "z", there)
    return [own, one, two, three, four]


def z_partner(which, z):
    return z ^ 1 if which == 0 else (((z + 1) ^ 1) + 7) & 7


def z_order(first, z):
    here = functools.partial(z_partner, first)
    there = functools.partial(z_partner, 1 - first)
    two = [there(z), here(there(z))]
    near = here(z)
    three = [there(near), here(there(near))]
    far = there(z)
    far_near = here(far)
    four = [there(far_near), here(there(far_near))]
    return [z, near] + two + three + four


def gather_xy(own):
    both = jnp.concatenate([own, lax.ppermute(own, "x", X_PAIRS)], axis=0)
    result = []
    for half in range(2):
        cols = both[:, half * 2 * HD : (half + 1) * 2 * HD]
        near = lax.ppermute(cols, "y", Y_PAIRS[half])
        far = lax.ppermute(jnp.concatenate([cols, near], axis=0), "y", Y_PAIRS[1 - half])
        result.append((near, far))
    return both, result


Y_STEPS = ((1, 3, 2), (3, 1, 2))


def attention_kernel(ids_ref, *refs):
    (q_both, near0, far0, near1, far1, k0, k1, k2, k3, k4, v0, v1, v2, v3, v4,
     out_ref, q_s, k_s, vt_s, v_s) = refs
    group = ids_ref[0]
    z = ids_ref[1]
    for half, (near, far) in enumerate(((near0, far0), (near1, far1))):
        first, second, third = Y_STEPS[half]
        for rel_y, ref, base, col in (
            (0, q_both, 0, half * 2 * HD),
            (first, near, 0, 0),
            (second, far, 0, 0),
            (third, far, 2 * PIECE, 0),
        ):
            for rel_x in range(NX):
                rows = slice(base + rel_x * PIECE, base + (rel_x + 1) * PIECE)
                for j in range(2):
                    q_s[half, rel_x * NY + rel_y, j * PIECE : (j + 1) * PIECE, :] = ref[
                        rows, col + j * HD : col + (j + 1) * HD
                    ]
    for first, pieces, dest in ((0, (k0, k1, k2, k3, k4), k_s), (1, (v0, v1, v2, v3, v4), v_s)):
        places = z_order(first, z)
        index = 0
        for piece in pieces:
            for part in range(piece.shape[0] // PIECE):
                start = pl.multiple_of(places[index] * PIECE, PIECE)
                dest[pl.ds(start, PIECE), :] = piece[part * PIECE : (part + 1) * PIECE, :]
                index += 1
    for half in range(2):
        vt_s[half] = jnp.transpose(v_s[:, half * HD : (half + 1) * HD])

    keys = NZ * PIECE

    def one(half, step, masked):
        query = q_s[half, step]
        scores = lax.dot_general(
            k_s[:, half * HD : (half + 1) * HD], query, NT, preferred_element_type=jnp.float32
        )
        if masked:
            key_row = lax.broadcasted_iota(jnp.int32, (keys, 2 * PIECE), 0)
            query_row = lax.broadcasted_iota(jnp.int32, (keys, 2 * PIECE), 1) % PIECE + z * PIECE
            scores = jnp.where(key_row <= query_row, scores, NEGATIVE)
        highest = jnp.max(scores, axis=0, keepdims=True)
        weights = jnp.exp2(scores - highest)
        total = jnp.sum(weights, axis=0, keepdims=True)
        summed = jnp.dot(vt_s[half], weights.astype(jnp.bfloat16), preferred_element_type=jnp.float32)
        normal = (summed / total).astype(jnp.bfloat16)
        level = highest + jnp.log2(total)
        top = level.astype(jnp.bfloat16)
        rest = level - top.astype(jnp.float32)
        middle = rest.astype(jnp.bfloat16)
        low = (rest - middle.astype(jnp.float32)).astype(jnp.bfloat16)
        for j in range(2):
            head = half * 2 + j
            lanes = slice(j * PIECE, (j + 1) * PIECE)
            out_ref[step, head * HD : (head + 1) * HD, :] = normal[:, lanes]
        return [part[:, j * PIECE : (j + 1) * PIECE] for j in range(2) for part in (top, middle, low)]

    def store_levels(step, rows):
        block = jnp.concatenate([r.astype(jnp.float32) for r in rows] + [jnp.zeros((4, PIECE), jnp.float32)], axis=0)
        out_ref[step, 4 * HD : 4 * HD + 16, :] = block.astype(jnp.bfloat16)

    store_levels(0, one(0, 0, True) + one(1, 0, True))

    def body(step, carry):
        seen = (group ^ step) > group

        @pl.when(seen)
        def _():
            store_levels(step, one(0, step, False) + one(1, step, False))

        @pl.when(jnp.logical_not(seen))
        def _():
            out_ref[step, 0 : 4 * HD, :] = jnp.zeros((4 * HD, PIECE), jnp.bfloat16)
            out_ref[step, 4 * HD : 4 * HD + 16, :] = jnp.full((16, PIECE), NEGATIVE, jnp.bfloat16)

        return carry

    lax.fori_loop(1, GROUP, body, 0)


def attention(ids, both, halves, keys, values):
    vmem = pl.BlockSpec(memory_space=pltpu.VMEM)
    smem = pl.BlockSpec(memory_space=pltpu.SMEM)
    (near0, far0), (near1, far1) = halves
    return pl.pallas_call(
        attention_kernel,
        out_shape=jax.ShapeDtypeStruct((GROUP, 4 * HD + 16, PIECE), jnp.bfloat16),
        in_specs=[smem] + [vmem] * 15,
        out_specs=vmem,
        scratch_shapes=[
            pltpu.VMEM((2, GROUP, 2 * PIECE, HD), jnp.bfloat16),
            pltpu.VMEM((NZ * PIECE, 2 * HD), jnp.bfloat16),
            pltpu.VMEM((2, HD, NZ * PIECE), jnp.bfloat16),
            pltpu.VMEM((NZ * PIECE, 2 * HD), jnp.bfloat16),
        ],
        compiler_params=pltpu.CompilerParams(vmem_limit_bytes=VMEM_LIMIT),
    )(ids, both, near0, far0, near1, far1, *keys, *values)


def combine_kernel(*refs):
    pieces, out_ref = refs[:-1], refs[-1]
    stats = [r[4 * HD : 4 * HD + 16, :].astype(jnp.float32) for r in pieces]
    for head in range(4):
        levels = [
            s[3 * head : 3 * head + 1] + s[3 * head + 1 : 3 * head + 2] + s[3 * head + 2 : 3 * head + 3]
            for s in stats
        ]
        highest = functools.reduce(jnp.maximum, levels)
        shares = [jnp.exp2(level - highest) for level in levels]
        scale = 1.0 / functools.reduce(jnp.add, shares)
        total = None
        for share, piece in zip(shares, pieces):
            term = piece[head * HD : (head + 1) * HD, :].astype(jnp.float32) * (share * scale)
            total = term if total is None else total + term
        out_ref[:, head * HD : (head + 1) * HD] = jnp.transpose(total).astype(jnp.bfloat16)


def combine(pieces):
    return pl.pallas_call(
        combine_kernel,
        out_shape=jax.ShapeDtypeStruct((PIECE, 4 * HD), jnp.bfloat16),
    )(*pieces)


def on_device(queries, keys, values, positions, query_gain, key_gain, out_weight):
    x, y, z = lax.axis_index("x"), lax.axis_index("y"), lax.axis_index("z")
    w, c = lax.axis_index("w"), lax.axis_index("c")
    ids = jnp.stack([x * NY + y, z]).astype(jnp.int32)
    query_rows, key_rows = prepare(queries, keys, positions, query_gain, key_gain)
    value_pieces = gather_z(values, 1)
    key_pieces = gather_z(key_rows, 0)
    both, halves = gather_xy(query_rows)
    partial = attention(ids, both, halves, key_pieces, value_pieces)
    received = [partial[0]] + [
        lax.ppermute(partial[step], ("x", "y"), pairs(GROUP, lambda i: i ^ step)) for step in range(1, GROUP)
    ]
    attended = combine(received)
    even = lax.ppermute(
        attended[: PIECE // 2], ("x", "y", "z"), pairs(64, lambda i: 2 * i if i < 32 else 127 - 2 * i)
    )
    odd = lax.ppermute(
        attended[PIECE // 2 :], ("x", "y", "z"), pairs(64, lambda i: 2 * i + 1 if i < 32 else 126 - 2 * i)
    )
    low = jnp.where(z % 2 == 0, even, odd)
    high = jnp.where(z % 2 == 0, odd, even)
    folded = jnp.stack([low, high]).reshape(2, 2, PIECE // 4, 4 * HD)
    mine = lax.dynamic_index_in_dim(folded, c, 1, keepdims=False)
    other = lax.dynamic_index_in_dim(folded, 1 - c, 1, keepdims=False)
    rows = jnp.concatenate([other, mine], axis=0).reshape(PIECE, 4 * HD)
    product = jnp.dot(rows, out_weight, preferred_element_type=jnp.float32).astype(jnp.bfloat16)
    product = product.reshape(2, 2, PIECE // 4, -1)
    got = lax.ppermute(product[0], "c", X_PAIRS)
    chip = product[1].astype(jnp.float32) + got.astype(jnp.float32)
    keep = lax.dynamic_index_in_dim(chip, w, 0, keepdims=False)
    give = lax.dynamic_index_in_dim(chip, 1 - w, 0, keepdims=False).astype(jnp.bfloat16)
    taken = lax.ppermute(give, "w", X_PAIRS)
    return (keep + taken.astype(jnp.float32)).astype(jnp.bfloat16)


def solution(mesh):
    inner = Mesh(mesh.devices.reshape(NX, NY, NZ, 2, 2), ("x", "y", "z", "w", "c"))
    ctx, head = ("x", "y", "z"), ("w", "c")
    return jax.shard_map(
        on_device,
        mesh=inner,
        in_specs=(P(ctx, head), P(ctx, head), P(ctx, head), P(ctx), P(), P(), P(head, None)),
        out_specs=P(ctx + head, None),
        check_vma=False,
    )
```

```python
import functools

import jax
import jax.numpy as jnp
import numpy as np
from jax import lax
from jax.experimental import pallas as pl
from jax.experimental.pallas import tpu as pltpu
from jax.sharding import Mesh
from jax.sharding import PartitionSpec as P

EPSILON = 1e-06
HD = 128
PIECE = 128
NX, NY, NZ = 2, 4, 8
GROUP = NX * NY
QUERY_FACTOR = float(168.0**-0.5 / np.log(2.0))
NEGATIVE = -1e30
FREQUENCY = (1000000.0 ** (-2.0 * np.arange(64, dtype=np.float64) / 128)).astype(np.float32)
VMEM_LIMIT = 48 * 1024 * 1024
NT = (((1,), (1,)), ((), ()))


def pairs(count, partner):
    return [(i, partner(i)) for i in range(count)]


Z_PAIRS = (pairs(NZ, lambda i: i ^ 1), pairs(NZ, lambda i: (((i + 1) ^ 1) + 7) % 8))
Y_PAIRS = (pairs(NY, lambda i: i ^ 1), pairs(NY, lambda i: i ^ 3))
X_PAIRS = pairs(NX, lambda i: i ^ 1)
BLOCK = 64


def prepare_kernel(ids_ref, q_ref, k_ref, v_ref, pos_ref, freq_ref, qg_ref, kg_ref, a_out, b_out, kv0_out, kv1_out):
    swapped = ids_ref[1] >= NZ // 2
    lane = lax.broadcasted_iota(jnp.int32, (PIECE, HD), 1)
    spread = jnp.broadcast_to(pos_ref[...].astype(jnp.float32), (PIECE, HD))
    angles = jnp.transpose(spread) * freq_ref[...]
    cosines = jnp.cos(angles)
    sines = jnp.where(lane < HD // 2, -1.0, 1.0) * jnp.sin(angles)

    def rotate(vector, gain):
        vector = vector.astype(jnp.float32)
        normed = vector * lax.rsqrt(jnp.mean(vector * vector, axis=-1, keepdims=True) + EPSILON) * gain
        return normed * cosines + pltpu.roll(normed, HD // 2, 1) * sines

    for head, out in enumerate((kv0_out, kv1_out)):
        cols = slice(head * HD, (head + 1) * HD)
        out[:, :HD] = rotate(k_ref[:, cols], kg_ref[...]).astype(jnp.bfloat16)
        out[:, HD:] = v_ref[:, cols]
    for head in range(4):
        cols = slice(head * HD, (head + 1) * HD)
        rows = rotate(q_ref[:, cols], qg_ref[...]) * QUERY_FACTOR
        first, second = rows[:BLOCK], rows[BLOCK:]
        a_out[:, cols] = jnp.where(swapped, second, first).astype(jnp.bfloat16)
        b_out[:, cols] = jnp.where(swapped, first, second).astype(jnp.bfloat16)


def prepare(ids, queries, keys, values, positions, query_gain, key_gain):
    freq = jnp.asarray(np.concatenate([FREQUENCY, FREQUENCY])[None, :])
    vmem = pl.BlockSpec(memory_space=pltpu.VMEM)
    smem = pl.BlockSpec(memory_space=pltpu.SMEM)
    block = jax.ShapeDtypeStruct((BLOCK, 4 * HD), jnp.bfloat16)
    key_value = jax.ShapeDtypeStruct((PIECE, 2 * HD), jnp.bfloat16)
    return pl.pallas_call(
        prepare_kernel,
        out_shape=(block, block, key_value, key_value),
        in_specs=[smem] + [vmem] * 7,
        out_specs=(vmem,) * 4,
    )(ids, queries, keys, values, positions[None, :], freq, query_gain[None, :], key_gain[None, :])


def gather_z(own, first):
    here, there = Z_PAIRS[first], Z_PAIRS[1 - first]
    one = lax.ppermute(own, "z", here)
    two = lax.ppermute(jnp.concatenate([own, one], axis=0), "z", there)
    three = lax.ppermute(two, "z", here)
    four = lax.ppermute(three, "z", there)
    return [own, one, two, three, four]


def z_partner(which, z):
    return z ^ 1 if which == 0 else (((z + 1) ^ 1) + 7) & 7


def z_order(first, z):
    here = functools.partial(z_partner, first)
    there = functools.partial(z_partner, 1 - first)
    two = [there(z), here(there(z))]
    near = here(z)
    three = [there(near), here(there(near))]
    far = there(z)
    far_near = here(far)
    four = [there(far_near), here(there(far_near))]
    return [z, near] + two + three + four


def folded_z(x, z, second):
    parity = (z >> 2) ^ second
    return (((z & 3) << 1) | parity) ^ (7 * x)


def fold_pairs(second, cross):
    moves = []
    for x in range(NX):
        for z in range(NZ):
            moves.append((x * NZ + z, (x ^ cross) * NZ + folded_z(x, z, second)))
    return moves


def gather_queries(a, b):
    blocks = [
        lax.ppermute(block, ("x", "z"), fold_pairs(second, cross))
        for cross in (0, 1)
        for second, block in ((0, a), (1, b))
    ]
    result = []
    for half in range(2):
        columns = slice(half * 2 * HD, (half + 1) * 2 * HD)
        own = jnp.concatenate([block[:, columns] for block in blocks], axis=0)
        near = lax.ppermute(own, "y", Y_PAIRS[half])
        far = lax.ppermute(jnp.concatenate([own, near], axis=0), "y", Y_PAIRS[1 - half])
        result += [own, near, far]
    return result


Y_STEPS = ((1, 3, 2), (3, 1, 2))


def attention_kernel(ids_ref, *refs):
    queries, pieces = refs[:6], (refs[6:11], refs[11:16])
    out_ref, q_s, k_s, vt_s, v_s = refs[16:]
    group = ids_ref[0]
    z = ids_ref[1]
    x, y = group >> 2, group & 3
    for half in range(2):
        own, near, far = queries[half * 3 : half * 3 + 3]
        first, second, third = Y_STEPS[half]
        for rel_y, ref, base in ((0, own, 0), (first, near, 0), (second, far, 0), (third, far, 2 * PIECE)):
            for rel_x in range(NX):
                rows = slice(base + rel_x * PIECE, base + (rel_x + 1) * PIECE)
                place = (x ^ rel_x) * NY + (y ^ rel_y)
                for j in range(2):
                    q_s[half, place, j] = ref[rows, j * HD : (j + 1) * HD]
        places = z_order(half, z)
        index = 0
        for piece in pieces[half]:
            for part in range(piece.shape[0] // PIECE):
                start = pl.multiple_of(places[index] * PIECE, PIECE)
                rows = slice(part * PIECE, (part + 1) * PIECE)
                k_s[half, pl.ds(start, PIECE), :] = piece[rows, :HD]
                v_s[half, pl.ds(start, PIECE), :] = piece[rows, HD:]
                index += 1
        vt_s[half] = jnp.transpose(v_s[half])

    keys = NZ * PIECE

    def one(half, step, masked):
        target = group ^ step
        outer = target >> 1
        shift = pl.multiple_of(((target ^ z) & 1) * BLOCK, BLOCK)
        rows = pl.ds(shift, BLOCK)
        query = jnp.concatenate(
            [q_s[half, source, j, rows, :] for j in range(2) for source in (outer, 7 - outer)], axis=0
        )
        scores = lax.dot_general(k_s[half], query, NT, preferred_element_type=jnp.float32)
        if masked:
            key_row = lax.broadcasted_iota(jnp.int32, (keys, 2 * PIECE), 0)
            lane = lax.broadcasted_iota(jnp.int32, (1, 2 * PIECE), 1)
            low = target * NZ + z
            block = jnp.where(lane % PIECE < BLOCK, low, 127 - low)
            last = block * BLOCK + lane % BLOCK - group * keys
            scores = jnp.where(key_row <= last, scores, NEGATIVE)
        highest = jnp.max(scores, axis=0, keepdims=True)
        weights = jnp.exp2(scores - highest)
        total = jnp.sum(weights, axis=0, keepdims=True)
        summed = jnp.dot(vt_s[half], weights.astype(jnp.bfloat16), preferred_element_type=jnp.float32)
        normal = (summed / total).astype(jnp.bfloat16)
        level = highest + jnp.log2(total)
        top = level.astype(jnp.bfloat16)
        rest = level - top.astype(jnp.float32)
        middle = rest.astype(jnp.bfloat16)
        low_part = (rest - middle.astype(jnp.float32)).astype(jnp.bfloat16)
        for j in range(2):
            head = half * 2 + j
            out_ref[step, head * HD : (head + 1) * HD, :] = normal[:, j * PIECE : (j + 1) * PIECE]
        return [part[:, j * PIECE : (j + 1) * PIECE] for j in range(2) for part in (top, middle, low_part)]

    def both(step, masked):
        rows = one(0, step, masked) + one(1, step, masked)
        block = jnp.concatenate([r.astype(jnp.float32) for r in rows] + [jnp.zeros((4, PIECE), jnp.float32)], axis=0)
        out_ref[step, 4 * HD : 4 * HD + 16, :] = block.astype(jnp.bfloat16)

    def body(step, carry):
        outer = (group ^ step) >> 1
        high = 7 - outer
        full = jnp.logical_and(outer > group, high > group)
        none = jnp.logical_and(outer < group, high < group)

        @pl.when(full)
        def _():
            both(step, False)

        @pl.when(jnp.logical_not(jnp.logical_or(full, none)))
        def _():
            both(step, True)

        @pl.when(none)
        def _():
            out_ref[step, 0 : 4 * HD, :] = jnp.zeros((4 * HD, PIECE), jnp.bfloat16)
            out_ref[step, 4 * HD : 4 * HD + 16, :] = jnp.full((16, PIECE), NEGATIVE, jnp.bfloat16)

        return carry

    lax.fori_loop(0, GROUP, body, 0)


def attention(ids, queries, pieces):
    vmem = pl.BlockSpec(memory_space=pltpu.VMEM)
    smem = pl.BlockSpec(memory_space=pltpu.SMEM)
    return pl.pallas_call(
        attention_kernel,
        out_shape=jax.ShapeDtypeStruct((GROUP, 4 * HD + 16, PIECE), jnp.bfloat16),
        in_specs=[smem] + [vmem] * 16,
        out_specs=vmem,
        scratch_shapes=[
            pltpu.VMEM((2, GROUP, 2, PIECE, HD), jnp.bfloat16),
            pltpu.VMEM((2, NZ * PIECE, HD), jnp.bfloat16),
            pltpu.VMEM((2, HD, NZ * PIECE), jnp.bfloat16),
            pltpu.VMEM((2, NZ * PIECE, HD), jnp.bfloat16),
        ],
        compiler_params=pltpu.CompilerParams(vmem_limit_bytes=VMEM_LIMIT),
    )(ids, *queries, *pieces[0], *pieces[1])


def combine_kernel(ids_ref, *refs):
    pieces, out_ref = refs[:-1], refs[-1]
    core = ids_ref[2]
    stats = [r[4 * HD : 4 * HD + 16, :].astype(jnp.float32) for r in pieces]
    quarter = PIECE // 4
    for head in range(4):
        levels = [
            s[3 * head : 3 * head + 1] + s[3 * head + 1 : 3 * head + 2] + s[3 * head + 2 : 3 * head + 3]
            for s in stats
        ]
        highest = functools.reduce(jnp.maximum, levels)
        shares = [jnp.exp2(level - highest) for level in levels]
        scale = 1.0 / functools.reduce(jnp.add, shares)
        total = None
        for share, piece in zip(shares, pieces):
            term = piece[head * HD : (head + 1) * HD, :].astype(jnp.float32) * (share * scale)
            total = term if total is None else total + term
        rows = jnp.transpose(total).astype(jnp.bfloat16)
        for k in range(4):
            own = 1 - ((k & 1) ^ core)
            start = pl.multiple_of(own * (PIECE // 2) + (k >> 1) * quarter, quarter)
            out_ref[pl.ds(start, quarter), head * HD : (head + 1) * HD] = rows[k * quarter : (k + 1) * quarter]


def combine(ids, pieces):
    vmem = pl.BlockSpec(memory_space=pltpu.VMEM)
    smem = pl.BlockSpec(memory_space=pltpu.SMEM)
    return pl.pallas_call(
        combine_kernel,
        out_shape=jax.ShapeDtypeStruct((PIECE, 4 * HD), jnp.bfloat16),
        in_specs=[smem] + [vmem] * GROUP,
        out_specs=vmem,
    )(ids, *pieces)


CHUNKS = 2


def project(rows, out_weight, w):
    chips = []
    width = out_weight.shape[1] // CHUNKS
    for chunk in range(CHUNKS):
        weight = out_weight[:, chunk * width : (chunk + 1) * width]
        product = jnp.dot(rows, weight, preferred_element_type=jnp.float32).astype(jnp.bfloat16)
        product = product.reshape(2, 2, PIECE // 4, width)
        got = lax.ppermute(product[0], "c", X_PAIRS)
        chip = product[1].astype(jnp.float32) + got.astype(jnp.float32)
        keep = lax.dynamic_index_in_dim(chip, w, 0, keepdims=False)
        give = lax.dynamic_index_in_dim(chip, 1 - w, 0, keepdims=False).astype(jnp.bfloat16)
        chips.append((keep, lax.ppermute(give, "w", X_PAIRS)))
    return jnp.concatenate([(keep + taken.astype(jnp.float32)).astype(jnp.bfloat16) for keep, taken in chips], axis=1)


def on_device(queries, keys, values, positions, query_gain, key_gain, out_weight):
    x, y, z = lax.axis_index("x"), lax.axis_index("y"), lax.axis_index("z")
    w, c = lax.axis_index("w"), lax.axis_index("c")
    ids = jnp.stack([x * NY + y, z, c]).astype(jnp.int32)
    a, b, kv0, kv1 = prepare(ids, queries, keys, values, positions, query_gain, key_gain)
    gathered = gather_queries(a, b)
    pieces = (gather_z(kv0, 0), gather_z(kv1, 1))
    partial = attention(ids, gathered, pieces)
    received = [partial[0]] + [
        lax.ppermute(partial[step], ("x", "y"), pairs(GROUP, lambda i: i ^ step)) for step in range(1, GROUP)
    ]
    return project(combine(ids, received), out_weight, w)


def solution(mesh):
    inner = Mesh(mesh.devices.reshape(NX, NY, NZ, 2, 2), ("x", "y", "z", "w", "c"))
    ctx, head = ("x", "y", "z"), ("w", "c")
    return jax.shard_map(
        on_device,
        mesh=inner,
        in_specs=(P(ctx, head), P(ctx, head), P(ctx, head), P(ctx), P(), P(), P(head, None)),
        out_specs=P(ctx + head, None),
        check_vma=False,
    )
```

```python
import functools

import jax
import jax.numpy as jnp
import numpy as np
from jax import lax
from jax.experimental import pallas as pl
from jax.experimental.pallas import tpu as pltpu
from jax.sharding import Mesh
from jax.sharding import PartitionSpec as P

EPSILON = 1e-06
HD = 128
PIECE = 128
NX, NY, NZ = 2, 4, 8
GROUP = NX * NY
QUERY_FACTOR = float(168.0**-0.5 / np.log(2.0))
NEGATIVE = -1e30
FREQUENCY = (1000000.0 ** (-2.0 * np.arange(64, dtype=np.float64) / 128)).astype(np.float32)
VMEM_LIMIT = 24 * 1024 * 1024
NT = (((1,), (1,)), ((), ()))


def pairs(count, partner):
    return [(i, partner(i)) for i in range(count)]


Z_PAIRS = (pairs(NZ, lambda i: i ^ 1), pairs(NZ, lambda i: (((i + 1) ^ 1) + 7) % 8))
Y_PAIRS = (pairs(NY, lambda i: i ^ 1), pairs(NY, lambda i: i ^ 3))
X_PAIRS = pairs(NX, lambda i: i ^ 1)
BLOCK = 64
STATS = 16
VMEM = pl.BlockSpec(memory_space=pltpu.VMEM)
SMEM = pl.BlockSpec(memory_space=pltpu.SMEM)


def rotate(vector, gain, cosines, sines):
    vector = vector.astype(jnp.float32)
    normed = vector * lax.rsqrt(jnp.mean(vector * vector, axis=-1, keepdims=True) + EPSILON) * gain
    return normed * cosines + pltpu.roll(normed, HD // 2, 1) * sines


def prepare_queries_kernel(q_ref, pos_ref, freq_ref, gain_ref, q_out, cos_out, sin_out):
    lane = lax.broadcasted_iota(jnp.int32, (PIECE, HD), 1)
    spread = jnp.broadcast_to(pos_ref[...].astype(jnp.float32), (PIECE, HD))
    angles = jnp.transpose(spread) * freq_ref[...]
    cosines = jnp.cos(angles)
    sines = jnp.where(lane < HD // 2, -1.0, 1.0) * jnp.sin(angles)
    cos_out[...] = cosines
    sin_out[...] = sines
    for head in range(4):
        cols = slice(head * HD, (head + 1) * HD)
        rows = rotate(q_ref[:, cols], gain_ref[...], cosines, sines)
        q_out[:, cols] = (rows * QUERY_FACTOR).astype(jnp.bfloat16)


def prepare_queries(queries, positions, gain):
    freq = jnp.asarray(np.concatenate([FREQUENCY, FREQUENCY])[None, :])
    table = jax.ShapeDtypeStruct((PIECE, HD), jnp.float32)
    return pl.pallas_call(
        prepare_queries_kernel,
        out_shape=(jax.ShapeDtypeStruct((PIECE, 4 * HD), jnp.bfloat16), table, table),
        in_specs=[VMEM] * 4,
        out_specs=(VMEM,) * 3,
    )(queries, positions[None, :], freq, gain[None, :])


def prepare_keys_kernel(k_ref, v_ref, cos_ref, sin_ref, gain_ref, kv0_out, kv1_out):
    for head, out in enumerate((kv0_out, kv1_out)):
        cols = slice(head * HD, (head + 1) * HD)
        rows = rotate(k_ref[:, cols], gain_ref[...], cos_ref[...], sin_ref[...])
        out[:, :HD] = rows.astype(jnp.bfloat16)
        out[:, HD:] = v_ref[:, cols]


def prepare_keys(keys, values, cosines, sines, gain):
    key_value = jax.ShapeDtypeStruct((PIECE, 2 * HD), jnp.bfloat16)
    return pl.pallas_call(
        prepare_keys_kernel,
        out_shape=(key_value, key_value),
        in_specs=[VMEM] * 5,
        out_specs=(VMEM,) * 2,
    )(keys, values, cosines, sines, gain[None, :])


def gather_z(own, first):
    here, there = Z_PAIRS[first], Z_PAIRS[1 - first]
    one = lax.ppermute(own, "z", here)
    two = lax.ppermute(jnp.concatenate([own, one], axis=0), "z", there)
    three = lax.ppermute(two, "z", here)
    four = lax.ppermute(three, "z", there)
    return [own, one, two, three, four]


def z_partner(which, z):
    return z ^ 1 if which == 0 else (((z + 1) ^ 1) + 7) & 7


def z_order(first, z):
    here = functools.partial(z_partner, first)
    there = functools.partial(z_partner, 1 - first)
    two = [there(z), here(there(z))]
    near = here(z)
    three = [there(near), here(there(near))]
    far = there(z)
    far_near = here(far)
    four = [there(far_near), here(there(far_near))]
    return [z, near] + two + three + four


def move_pairs():
    return [(x * NZ + z, x * NZ + ((((z & 3) ^ (3 * x)) << 1) | (z >> 2))) for x in range(NX) for z in range(NZ)]


def gather_xy(own):
    both = jnp.concatenate([own, lax.ppermute(own, "x", X_PAIRS)], axis=0)
    result = [both]
    for half in range(2):
        cols = both[:, half * 2 * HD : (half + 1) * 2 * HD]
        near = lax.ppermute(cols, "y", Y_PAIRS[half])
        far = lax.ppermute(jnp.concatenate([cols, near], axis=0), "y", Y_PAIRS[1 - half])
        result += [near, far]
    return result


Y_STEPS = ((1, 3, 2), (3, 1, 2))


def attention_kernel(ids_ref, *refs):
    own, pieces = refs[0], (refs[5:10], refs[10:15])
    out_ref, q_s, k_s, v_s, level_s = refs[15:]
    group, z, w = ids_ref[0], ids_ref[1], ids_ref[3]
    x, y = group >> 2, group & 3
    for half in range(2):
        near, far = refs[1 + 2 * half], refs[2 + 2 * half]
        first, second, third = Y_STEPS[half]
        for rel_y, ref, base, col in (
            (0, own, 0, half * 2 * HD),
            (first, near, 0, 0),
            (second, far, 0, 0),
            (third, far, 2 * PIECE, 0),
        ):
            for rel_x in range(NX):
                rows = slice(base + rel_x * PIECE, base + (rel_x + 1) * PIECE)
                place = (x ^ rel_x) * NY + (y ^ rel_y)
                for j in range(2):
                    q_s[half, place, j] = ref[rows, col + j * HD : col + (j + 1) * HD]
        places = z_order(half, z)
        index = 0
        for piece in pieces[half]:
            for part in range(piece.shape[0] // PIECE):
                start = pl.multiple_of(places[index] * PIECE, PIECE)
                rows = slice(part * PIECE, (part + 1) * PIECE)
                k_s[half, pl.ds(start, PIECE), :] = piece[rows, :HD]
                v_s[half, pl.ds(start, PIECE), :] = piece[rows, HD:]
                index += 1
    level_s[...] = jnp.full((PIECE, HD), NEGATIVE, jnp.float32)

    keys = NZ * PIECE
    width = 4 * PIECE

    def slot(source):
        upper = source >> 2
        end_x = ((source >> 1) & 1) ^ w
        end_y = (((source & 1) ^ upper) << 1) | ((z & 1) ^ upper)
        return group ^ ((end_x << 2) | end_y)

    def one(half, pair, masked):
        query = q_s[half, pl.ds(pair * 2, 2)].reshape(width, HD)
        scores = lax.dot_general(query, k_s[half], NT, preferred_element_type=jnp.float32)
        if masked:
            row = lax.broadcasted_iota(jnp.int32, (width, 1), 0)
            source = pair * 2 + row // (2 * PIECE)
            at_z = ((z & 1) << 2) | ((z >> 1) ^ (3 * (source >> 2)))
            last = (source * NZ + at_z) * PIECE + row % PIECE - group * keys
            column = lax.broadcasted_iota(jnp.int32, (width, keys), 1)
            scores = jnp.where(column <= last, scores, NEGATIVE)
        highest = jnp.max(scores, axis=1, keepdims=True)
        weights = jnp.exp2(scores - highest)
        total = jnp.sum(weights, axis=1, keepdims=True)
        summed = jnp.dot(weights.astype(jnp.bfloat16), v_s[half], preferred_element_type=jnp.float32)
        normal = (summed / total).astype(jnp.bfloat16)
        level = highest + jnp.log2(total)
        lane = lax.broadcasted_iota(jnp.int32, (PIECE, HD), 1)
        for r in range(2):
            step = slot(pair * 2 + r)
            for j in range(2):
                base = (r * 2 + j) * PIECE
                head = half * 2 + j
                out_ref[step, :PIECE, head * HD : (head + 1) * HD] = normal[base : base + PIECE]
                level_s[...] = jnp.where(lane == step * 4 + head, level[base : base + PIECE], level_s[...])

    def body(pair, carry):
        full = pair * 2 > group
        none = pair * 2 + 1 < group

        @pl.when(full)
        def _():
            one(0, pair, False)
            one(1, pair, False)

        @pl.when(jnp.logical_not(jnp.logical_or(full, none)))
        def _():
            one(0, pair, True)
            one(1, pair, True)

        @pl.when(none)
        def _():
            for r in range(2):
                out_ref[slot(pair * 2 + r), :PIECE, :] = jnp.zeros((PIECE, 4 * HD), jnp.bfloat16)

        return carry

    lax.fori_loop(0, GROUP // 2, body, 0)
    levels = jnp.transpose(level_s[...])
    row = lax.broadcasted_iota(jnp.int32, (STATS, PIECE), 0)
    for step in range(GROUP):
        for head in range(4):
            line = jnp.broadcast_to(levels[step * 4 + head : step * 4 + head + 1], (STATS, PIECE))
            top = line.astype(jnp.bfloat16).astype(jnp.float32)
            middle = (line - top).astype(jnp.bfloat16).astype(jnp.float32)
            rest = line - top - middle
            stats = jnp.where(row == 0, top, jnp.where(row == 1, middle, jnp.where(row == 2, rest, 0.0)))
            out_ref[step, PIECE:, head * HD : (head + 1) * HD] = stats.astype(jnp.bfloat16)


def attention(ids, queries, pieces):
    flops = 2 * 2 * 4 * GROUP * PIECE * NZ * PIECE * HD
    return pl.pallas_call(
        attention_kernel,
        out_shape=jax.ShapeDtypeStruct((GROUP, PIECE + STATS, 4 * HD), jnp.bfloat16),
        in_specs=[SMEM] + [VMEM] * 15,
        out_specs=VMEM,
        scratch_shapes=[
            pltpu.VMEM((2, GROUP, 2, PIECE, HD), jnp.bfloat16),
            pltpu.VMEM((2, NZ * PIECE, HD), jnp.bfloat16),
            pltpu.VMEM((2, NZ * PIECE, HD), jnp.bfloat16),
            pltpu.VMEM((PIECE, HD), jnp.float32),
        ],
        compiler_params=pltpu.CompilerParams(vmem_limit_bytes=VMEM_LIMIT),
        cost_estimate=pl.CostEstimate(flops=flops, bytes_accessed=2**22, transcendentals=2**22),
    )(ids, *queries, *pieces[0], *pieces[1])


def combine_kernel(ids_ref, partial, *refs):
    pieces = [partial.at[0]] + list(refs[: GROUP - 1])
    keep_out, give_out = refs[GROUP - 1 :]
    second_stays = (ids_ref[0] & 1) == 1
    stats = [piece[PIECE:, :].astype(jnp.float32) for piece in pieces]
    levels = [s[0:1] + s[1:2] + s[2:3] for s in stats]
    highest = functools.reduce(jnp.maximum, levels)
    shares = [jnp.exp2(level - highest) for level in levels]
    scale = 1.0 / functools.reduce(jnp.add, shares)
    table = jnp.concatenate([share * scale for share in shares], axis=0)
    for head in range(4):
        lanes = slice(head * HD, (head + 1) * HD)
        columns = jnp.transpose(table[:, lanes])
        totals = []
        for first in (0, BLOCK):
            rows = slice(first, first + BLOCK)
            total = None
            for s in range(GROUP):
                term = pieces[s][rows, lanes].astype(jnp.float32) * columns[rows, s : s + 1]
                total = term if total is None else total + term
            totals.append(total)
        keep_out[:, lanes] = jnp.where(second_stays, totals[1], totals[0]).astype(jnp.bfloat16)
        give_out[:, lanes] = jnp.where(second_stays, totals[0], totals[1]).astype(jnp.bfloat16)


def combine(ids, partial, received):
    block = jax.ShapeDtypeStruct((BLOCK, 4 * HD), jnp.bfloat16)
    return pl.pallas_call(
        combine_kernel,
        out_shape=(block, block),
        in_specs=[SMEM] + [VMEM] * GROUP,
        out_specs=(VMEM, VMEM),
    )(ids, partial, *received)


TILE = 768


def project_kernel(ids_ref, kept, taken, weight, other_out, mine_out, rows_s):
    core = ids_ref[2]
    quarter = PIECE // 4
    kept_high = ((ids_ref[0] ^ ids_ref[1]) & 1) == 1
    first, second = kept[...], taken[...]
    low = jnp.where(kept_high, second, first)
    high = jnp.where(kept_high, first, second)
    for k, block in enumerate((low, high)):
        for part in range(2):
            own = 1 - (part ^ core)
            start = pl.multiple_of(own * BLOCK + k * quarter, quarter)
            rows_s[pl.ds(start, quarter), :] = block[part * quarter : (part + 1) * quarter]
    rows = rows_s[...]
    for tile in range(weight.shape[1] // TILE):
        lanes = slice(tile * TILE, (tile + 1) * TILE)
        product = jnp.dot(rows, weight[:, lanes], preferred_element_type=jnp.float32).astype(jnp.bfloat16)
        other_out[:, lanes] = product[:BLOCK]
        mine_out[:, lanes] = product[BLOCK:]


def project(ids, kept, taken, out_weight):
    half = jax.ShapeDtypeStruct((BLOCK, out_weight.shape[1]), jnp.bfloat16)
    return pl.pallas_call(
        project_kernel,
        out_shape=(half, half),
        in_specs=[SMEM] + [VMEM] * 3,
        out_specs=(VMEM, VMEM),
        scratch_shapes=[pltpu.VMEM((PIECE, 4 * HD), jnp.bfloat16)],
        compiler_params=pltpu.CompilerParams(vmem_limit_bytes=VMEM_LIMIT),
        cost_estimate=pl.CostEstimate(flops=2 * PIECE * 512 * 5376, bytes_accessed=2**23, transcendentals=0),
    )(ids, kept, taken, out_weight)


def on_device(queries, keys, values, positions, query_gain, key_gain, out_weight):
    x, y, z = lax.axis_index("x"), lax.axis_index("y"), lax.axis_index("z")
    w, c = lax.axis_index("w"), lax.axis_index("c")
    ids = jnp.stack([x * NY + y, z, c, w]).astype(jnp.int32)
    query_rows, cosines, sines = prepare_queries(queries, positions, query_gain)
    moved = lax.ppermute(query_rows, ("x", "z"), move_pairs())
    kv0, kv1 = prepare_keys(keys, values, cosines, sines, key_gain)
    pieces = (gather_z(kv0, 0), gather_z(kv1, 1))
    partial = attention(ids, gather_xy(moved), pieces)
    received = [
        lax.ppermute(partial[step], ("x", "y"), pairs(GROUP, lambda i: i ^ step)) for step in range(1, GROUP)
    ]
    kept, given = combine(ids, partial, received)
    taken = lax.ppermute(given, "z", Z_PAIRS[0])
    other, mine = project(ids, kept, taken, out_weight)
    got = lax.ppermute(other, "c", X_PAIRS)
    chip = (mine.astype(jnp.float32) + got.astype(jnp.float32)).reshape(2, PIECE // 4, -1)
    keep = lax.dynamic_index_in_dim(chip, w, 0, keepdims=False)
    give = lax.dynamic_index_in_dim(chip, 1 - w, 0, keepdims=False).astype(jnp.bfloat16)
    landed = lax.ppermute(give, ("x", "w"), pairs(4, lambda i: i ^ 3))
    return (keep + landed.astype(jnp.float32)).astype(jnp.bfloat16)


def solution(mesh):
    inner = Mesh(mesh.devices.reshape(NX, NY, NZ, 2, 2), ("x", "y", "z", "w", "c"))
    ctx, head = ("x", "y", "z"), ("w", "c")
    return jax.shard_map(
        on_device,
        mesh=inner,
        in_specs=(P(ctx, head), P(ctx, head), P(ctx, head), P(ctx), P(), P(), P(head, None)),
        out_specs=P(ctx + head, None),
        check_vma=False,
    )
```

```python
import functools

import jax
import jax.numpy as jnp
import numpy as np
from jax import lax
from jax.experimental import pallas as pl
from jax.experimental.pallas import tpu as pltpu
from jax.sharding import Mesh
from jax.sharding import PartitionSpec as P

EPSILON = 1e-06
HD = 128
PIECE = 128
NX, NY, NZ = 2, 4, 8
GROUP = NX * NY
QUERY_FACTOR = float(168.0**-0.5 / np.log(2.0))
NEGATIVE = -1e30
FREQUENCY = (1000000.0 ** (-2.0 * np.arange(64, dtype=np.float64) / 128)).astype(np.float32)
VMEM_LIMIT = 24 * 1024 * 1024
NT = (((1,), (1,)), ((), ()))


def pairs(count, partner):
    return [(i, partner(i)) for i in range(count)]


def z_partner(which, z):
    return z ^ 1 if which == 0 else (((z + 1) ^ 1) + 7) & 7


def y_partner(which, y):
    return y ^ (1, 3)[which]


def by_core(count, partner):
    return tuple(
        [(i * 2 + core, partner(core ^ turn, i) * 2 + core) for i in range(count) for core in range(2)] for turn in range(2)
    )


Z_PAIRS = by_core(NZ, z_partner)
Y_PAIRS = by_core(NY, y_partner)
X_PAIRS = pairs(NX, lambda i: i ^ 1)
BLOCK = 64
STATS = 16
VMEM = pl.BlockSpec(memory_space=pltpu.VMEM)
SMEM = pl.BlockSpec(memory_space=pltpu.SMEM)


def rotate(vector, gain, cosines, sines):
    vector = vector.astype(jnp.float32)
    normed = vector * lax.rsqrt(jnp.mean(vector * vector, axis=-1, keepdims=True) + EPSILON) * gain
    return normed * cosines + pltpu.roll(normed, HD // 2, 1) * sines


def prepare_queries_kernel(q_ref, pos_ref, freq_ref, gain_ref, q_out, cos_out, sin_out):
    lane = lax.broadcasted_iota(jnp.int32, (PIECE, HD), 1)
    spread = jnp.broadcast_to(pos_ref[...].astype(jnp.float32), (PIECE, HD))
    angles = jnp.transpose(spread) * freq_ref[...]
    cosines = jnp.cos(angles)
    sines = jnp.where(lane < HD // 2, -1.0, 1.0) * jnp.sin(angles)
    cos_out[...] = cosines
    sin_out[...] = sines
    for head in range(4):
        cols = slice(head * HD, (head + 1) * HD)
        rows = rotate(q_ref[:, cols], gain_ref[...], cosines, sines)
        q_out[:, cols] = (rows * QUERY_FACTOR).astype(jnp.bfloat16)


def prepare_queries(queries, positions, gain):
    freq = jnp.asarray(np.concatenate([FREQUENCY, FREQUENCY])[None, :])
    table = jax.ShapeDtypeStruct((PIECE, HD), jnp.float32)
    return pl.pallas_call(
        prepare_queries_kernel,
        out_shape=(jax.ShapeDtypeStruct((PIECE, 4 * HD), jnp.bfloat16), table, table),
        in_specs=[VMEM] * 4,
        out_specs=(VMEM,) * 3,
    )(queries, positions[None, :], freq, gain[None, :])


def prepare_keys_kernel(k_ref, v_ref, cos_ref, sin_ref, gain_ref, out):
    for head in range(2):
        cols = slice(head * HD, (head + 1) * HD)
        rows = rotate(k_ref[:, cols], gain_ref[...], cos_ref[...], sin_ref[...])
        out[:, cols] = rows.astype(jnp.bfloat16)
    out[:, 2 * HD :] = v_ref[...]


def prepare_keys(keys, values, cosines, sines, gain):
    return pl.pallas_call(
        prepare_keys_kernel,
        out_shape=jax.ShapeDtypeStruct((PIECE, 4 * HD), jnp.bfloat16),
        in_specs=[VMEM] * 5,
        out_specs=VMEM,
    )(keys, values, cosines, sines, gain[None, :])


def gather_z(own):
    here, there = Z_PAIRS
    one = lax.ppermute(own, ("z", "c"), here)
    two = lax.ppermute(jnp.concatenate([own, one], axis=0), ("z", "c"), there)
    three = lax.ppermute(two, ("z", "c"), here)
    four = lax.ppermute(three, ("z", "c"), there)
    return [own, one, two, three, four]


def z_order(core, z):
    def step(which, place):
        return jnp.where(which == 0, z_partner(0, place), z_partner(1, place))

    def here(place):
        return step(core, place)

    def there(place):
        return step(1 - core, place)

    far, near = there(z), here(z)
    two = [far, here(far)]
    three = [there(near), here(there(near))]
    four = [there(here(far)), here(there(here(far)))]
    return [z, near] + two + three + four


def move_pairs():
    return [(x * NZ + z, x * NZ + ((((z & 3) ^ (3 * x)) << 1) | (z >> 2))) for x in range(NX) for z in range(NZ)]


def gather_xy(own):
    both = jnp.concatenate([own, lax.ppermute(own, "x", X_PAIRS)], axis=0)
    near = lax.ppermute(both, ("y", "c"), Y_PAIRS[0])
    far = lax.ppermute(jnp.concatenate([both, near], axis=0), ("y", "c"), Y_PAIRS[1])
    return both, near, far


def attention_kernel(ids_ref, *refs):
    own, near, far = refs[:3]
    pieces = refs[3:8]
    out_ref, q_s, k_s, v_s, level_s = refs[8:]
    group, z, core, w = ids_ref[0], ids_ref[1], ids_ref[2], ids_ref[3]
    x, y = group >> 2, group & 3
    first = 1 + 2 * core
    for rel_y, ref, base in ((0, own, 0), (first, near, 0), (4 - first, far, 0), (2, far, 2 * PIECE)):
        for rel_x in range(NX):
            rows = slice(base + rel_x * PIECE, base + (rel_x + 1) * PIECE)
            place = (x ^ rel_x) * NY + (y ^ rel_y)
            for head in range(4):
                q_s[head // 2, place, head % 2] = ref[rows, head * HD : (head + 1) * HD]
    places = z_order(core, z)
    index = 0
    for piece in pieces:
        for part in range(piece.shape[0] // PIECE):
            start = pl.multiple_of(places[index] * PIECE, PIECE)
            rows = slice(part * PIECE, (part + 1) * PIECE)
            for half in range(2):
                k_s[half, pl.ds(start, PIECE), :] = piece[rows, half * HD : (half + 1) * HD]
                v_s[half, pl.ds(start, PIECE), :] = piece[rows, (2 + half) * HD : (3 + half) * HD]
            index += 1
    level_s[...] = jnp.full((PIECE, HD), NEGATIVE, jnp.float32)

    keys = NZ * PIECE
    width = 4 * PIECE

    def slot(source):
        upper = source >> 2
        end_x = ((source >> 1) & 1) ^ w
        end_y = (((source & 1) ^ upper) << 1) | ((z & 1) ^ upper)
        return group ^ ((end_x << 2) | end_y)

    def one(half, pair, masked):
        query = q_s[half, pl.ds(pair * 2, 2)].reshape(width, HD)
        scores = lax.dot_general(query, k_s[half], NT, preferred_element_type=jnp.float32)
        if masked:
            row = lax.broadcasted_iota(jnp.int32, (width, 1), 0)
            source = pair * 2 + row // (2 * PIECE)
            at_z = ((z & 1) << 2) | ((z >> 1) ^ (3 * (source >> 2)))
            last = (source * NZ + at_z) * PIECE + row % PIECE - group * keys
            column = lax.broadcasted_iota(jnp.int32, (width, keys), 1)
            scores = jnp.where(column <= last, scores, NEGATIVE)
        highest = jnp.max(scores, axis=1, keepdims=True)
        weights = jnp.exp2(scores - highest)
        total = jnp.sum(weights, axis=1, keepdims=True)
        summed = jnp.dot(weights.astype(jnp.bfloat16), v_s[half], preferred_element_type=jnp.float32)
        normal = (summed / total).astype(jnp.bfloat16)
        level = highest + jnp.log2(total)
        lane = lax.broadcasted_iota(jnp.int32, (PIECE, HD), 1)
        for r in range(2):
            step = slot(pair * 2 + r)
            for j in range(2):
                base = (r * 2 + j) * PIECE
                head = half * 2 + j
                out_ref[step, :PIECE, head * HD : (head + 1) * HD] = normal[base : base + PIECE]
                level_s[...] = jnp.where(lane == step * 4 + head, level[base : base + PIECE], level_s[...])

    def body(pair, carry):
        full = pair * 2 > group
        none = pair * 2 + 1 < group

        @pl.when(full)
        def _():
            one(0, pair, False)
            one(1, pair, False)

        @pl.when(jnp.logical_not(jnp.logical_or(full, none)))
        def _():
            one(0, pair, True)
            one(1, pair, True)

        @pl.when(none)
        def _():
            for r in range(2):
                out_ref[slot(pair * 2 + r), :PIECE, :] = jnp.zeros((PIECE, 4 * HD), jnp.bfloat16)

        return carry

    lax.fori_loop(0, GROUP // 2, body, 0)
    levels = jnp.transpose(level_s[...])
    row = lax.broadcasted_iota(jnp.int32, (STATS, PIECE), 0)
    for step in range(GROUP):
        for head in range(4):
            line = jnp.broadcast_to(levels[step * 4 + head : step * 4 + head + 1], (STATS, PIECE))
            top = line.astype(jnp.bfloat16).astype(jnp.float32)
            middle = (line - top).astype(jnp.bfloat16).astype(jnp.float32)
            rest = line - top - middle
            stats = jnp.where(row == 0, top, jnp.where(row == 1, middle, jnp.where(row == 2, rest, 0.0)))
            out_ref[step, PIECE:, head * HD : (head + 1) * HD] = stats.astype(jnp.bfloat16)


def attention(ids, queries, pieces):
    flops = 2 * 2 * 4 * GROUP * PIECE * NZ * PIECE * HD
    return pl.pallas_call(
        attention_kernel,
        out_shape=jax.ShapeDtypeStruct((GROUP, PIECE + STATS, 4 * HD), jnp.bfloat16),
        in_specs=[SMEM] + [VMEM] * 8,
        out_specs=VMEM,
        scratch_shapes=[
            pltpu.VMEM((2, GROUP, 2, PIECE, HD), jnp.bfloat16),
            pltpu.VMEM((2, NZ * PIECE, HD), jnp.bfloat16),
            pltpu.VMEM((2, NZ * PIECE, HD), jnp.bfloat16),
            pltpu.VMEM((PIECE, HD), jnp.float32),
        ],
        compiler_params=pltpu.CompilerParams(vmem_limit_bytes=VMEM_LIMIT),
        cost_estimate=pl.CostEstimate(flops=flops, bytes_accessed=2**22, transcendentals=2**22),
    )(ids, *queries, *pieces)


def combine_kernel(ids_ref, partial, *refs):
    pieces = [partial.at[0]] + list(refs[: GROUP - 1])
    keep_out, give_out = refs[GROUP - 1 :]
    second_stays = (ids_ref[0] & 1) == 1
    stats = [piece[PIECE:, :].astype(jnp.float32) for piece in pieces]
    levels = [s[0:1] + s[1:2] + s[2:3] for s in stats]
    highest = functools.reduce(jnp.maximum, levels)
    shares = [jnp.exp2(level - highest) for level in levels]
    scale = 1.0 / functools.reduce(jnp.add, shares)
    table = jnp.concatenate([share * scale for share in shares], axis=0)
    for head in range(4):
        lanes = slice(head * HD, (head + 1) * HD)
        columns = jnp.transpose(table[:, lanes])
        totals = []
        for first in (0, BLOCK):
            rows = slice(first, first + BLOCK)
            total = None
            for s in range(GROUP):
                term = pieces[s][rows, lanes].astype(jnp.float32) * columns[rows, s : s + 1]
                total = term if total is None else total + term
            totals.append(total)
        keep_out[:, lanes] = jnp.where(second_stays, totals[1], totals[0]).astype(jnp.bfloat16)
        give_out[:, lanes] = jnp.where(second_stays, totals[0], totals[1]).astype(jnp.bfloat16)


def combine(ids, partial, received):
    block = jax.ShapeDtypeStruct((BLOCK, 4 * HD), jnp.bfloat16)
    return pl.pallas_call(
        combine_kernel,
        out_shape=(block, block),
        in_specs=[SMEM] + [VMEM] * GROUP,
        out_specs=(VMEM, VMEM),
    )(ids, partial, *received)


def project(block, out_weight, c):
    product = jnp.dot(block, out_weight, preferred_element_type=jnp.float32).astype(jnp.bfloat16)
    product = product.reshape(2, PIECE // 4, -1)
    mine = lax.dynamic_index_in_dim(product, c, 0, keepdims=False)
    other = lax.dynamic_index_in_dim(product, 1 - c, 0, keepdims=False)
    return mine.astype(jnp.float32) + lax.ppermute(other, "c", X_PAIRS).astype(jnp.float32)


def on_device(queries, keys, values, positions, query_gain, key_gain, out_weight):
    x, y, z = lax.axis_index("x"), lax.axis_index("y"), lax.axis_index("z")
    w, c = lax.axis_index("w"), lax.axis_index("c")
    ids = jnp.stack([x * NY + y, z, c, w]).astype(jnp.int32)
    query_rows, cosines, sines = prepare_queries(queries, positions, query_gain)
    moved = lax.ppermute(query_rows, ("x", "z"), move_pairs())
    pieces = gather_z(prepare_keys(keys, values, cosines, sines, key_gain))
    partial = attention(ids, gather_xy(moved), pieces)
    received = [
        lax.ppermute(partial[step], ("x", "y"), pairs(GROUP, lambda i: i ^ step)) for step in range(1, GROUP)
    ]
    kept, given = combine(ids, partial, received)
    taken = lax.ppermute(given, "z", pairs(NZ, lambda i: i ^ 1))
    sums = [project(block, out_weight, c) for block in (kept, taken)]
    own_kept = ((y ^ z) & 1) == w
    keep = jnp.where(own_kept, sums[0], sums[1])
    give = jnp.where(own_kept, sums[1], sums[0]).astype(jnp.bfloat16)
    landed = lax.ppermute(give, ("x", "w"), pairs(4, lambda i: i ^ 3))
    return (keep + landed.astype(jnp.float32)).astype(jnp.bfloat16)


def solution(mesh):
    inner = Mesh(mesh.devices.reshape(NX, NY, NZ, 2, 2), ("x", "y", "z", "w", "c"))
    ctx, head = ("x", "y", "z"), ("w", "c")
    return jax.shard_map(
        on_device,
        mesh=inner,
        in_specs=(P(ctx, head), P(ctx, head), P(ctx, head), P(ctx), P(), P(), P(head, None)),
        out_specs=P(ctx + head, None),
        check_vma=False,
    )
```

```python
import functools

import jax
import jax.numpy as jnp
import numpy as np
from jax import lax
from jax.experimental import pallas as pl
from jax.experimental.pallas import tpu as pltpu
from jax.sharding import Mesh
from jax.sharding import PartitionSpec as P

EPSILON = 1e-06
HD = 128
PIECE = 128
NX, NY, NZ = 2, 4, 8
GROUP = NX * NY
QUERY_FACTOR = float(168.0**-0.5 / np.log(2.0))
NEGATIVE = -1e30
FREQUENCY = (1000000.0 ** (-2.0 * np.arange(64, dtype=np.float64) / 128)).astype(np.float32)
VMEM_LIMIT = 16 * 1024 * 1024
SMALL = pltpu.CompilerParams(vmem_limit_bytes=8 * 1024 * 1024)
NT = (((1,), (1,)), ((), ()))


def pairs(count, partner):
    return [(i, partner(i)) for i in range(count)]


def z_partner(which, z):
    return z ^ 1 if which == 0 else (((z + 1) ^ 1) + 7) & 7


def y_partner(which, y):
    return y ^ (1, 3)[which]


def by_core(count, partner):
    return tuple(
        [(i * 2 + core, partner(core ^ turn, i) * 2 + core) for i in range(count) for core in range(2)] for turn in range(2)
    )


Z_PAIRS = by_core(NZ, z_partner)
Y_PAIRS = by_core(NY, y_partner)
X_PAIRS = pairs(NX, lambda i: i ^ 1)
BLOCK = 64
STATS = 16
VMEM = pl.BlockSpec(memory_space=pltpu.VMEM)
SMEM = pl.BlockSpec(memory_space=pltpu.SMEM)


def rotate(vector, gain, cosines, sines):
    vector = vector.astype(jnp.float32)
    normed = vector * lax.rsqrt(jnp.mean(vector * vector, axis=-1, keepdims=True) + EPSILON) * gain
    return normed * cosines + pltpu.roll(normed, HD // 2, 1) * sines


def prepare_keys_kernel(k_ref, v_ref, pos_ref, freq_ref, gain_ref, out, cos_out, sin_out):
    lane = lax.broadcasted_iota(jnp.int32, (PIECE, HD), 1)
    spread = jnp.broadcast_to(pos_ref[...].astype(jnp.float32), (PIECE, HD))
    angles = jnp.transpose(spread) * freq_ref[...]
    cosines = jnp.cos(angles)
    sines = jnp.where(lane < HD // 2, -1.0, 1.0) * jnp.sin(angles)
    cos_out[...] = cosines
    sin_out[...] = sines
    for head in range(2):
        cols = slice(head * HD, (head + 1) * HD)
        rows = rotate(k_ref[:, cols], gain_ref[...], cosines, sines)
        out[:, cols] = rows.astype(jnp.bfloat16)
    out[:, 2 * HD :] = v_ref[...]


def prepare_keys(keys, values, positions, gain):
    freq = jnp.asarray(np.concatenate([FREQUENCY, FREQUENCY])[None, :])
    table = jax.ShapeDtypeStruct((PIECE, HD), jnp.float32)
    return pl.pallas_call(
        prepare_keys_kernel,
        out_shape=(jax.ShapeDtypeStruct((PIECE, 4 * HD), jnp.bfloat16), table, table),
        in_specs=[VMEM] * 5,
        out_specs=(VMEM,) * 3,
    )(keys, values, positions[None, :], freq, gain[None, :])


def prepare_queries_kernel(q_ref, cos_ref, sin_ref, gain_ref, out):
    for head in range(4):
        cols = slice(head * HD, (head + 1) * HD)
        rows = rotate(q_ref[:, cols], gain_ref[...], cos_ref[...], sin_ref[...])
        out[:, cols] = (rows * QUERY_FACTOR).astype(jnp.bfloat16)


def prepare_queries(queries, cosines, sines, gain):
    return pl.pallas_call(
        prepare_queries_kernel,
        out_shape=jax.ShapeDtypeStruct((PIECE, 4 * HD), jnp.bfloat16),
        in_specs=[VMEM] * 4,
        out_specs=VMEM,
    )(queries, cosines, sines, gain[None, :])


def gather_z(own):
    here, there = Z_PAIRS
    one = lax.ppermute(own, ("z", "c"), here)
    two = lax.ppermute(jnp.concatenate([own, one], axis=0), ("z", "c"), there)
    three = lax.ppermute(two, ("z", "c"), here)
    four = lax.ppermute(three, ("z", "c"), there)
    return [own, one, two, three, four]


def z_order(core, z):
    def step(which, place):
        return jnp.where(which == 0, z_partner(0, place), z_partner(1, place))

    def here(place):
        return step(core, place)

    def there(place):
        return step(1 - core, place)

    far, near = there(z), here(z)
    two = [far, here(far)]
    three = [there(near), here(there(near))]
    four = [there(here(far)), here(there(here(far)))]
    return [z, near] + two + three + four


def move_pairs():
    return [(x * NZ + z, x * NZ + ((((z & 3) ^ (3 * x)) << 1) | (z >> 2))) for x in range(NX) for z in range(NZ)]


def gather_xy(own):
    both = jnp.concatenate([own, lax.ppermute(own, "x", X_PAIRS)], axis=0)
    near = lax.ppermute(both, ("y", "c"), Y_PAIRS[0])
    far = lax.ppermute(jnp.concatenate([both, near], axis=0), ("y", "c"), Y_PAIRS[1])
    return both, near, far


def turned(step):
    return (4 * (step & 1)) ^ ((step >> 1) & 1) ^ (3 * ((step >> 2) & 1))


def position(core, step):
    back = (2 * (step & 1)) ^ (6 * ((step >> 1) & 1)) ^ ((step >> 2) & 1)
    return jnp.where(core == 0, step, back)


def exchange(partial):
    received = []
    for k in range(1, GROUP):
        moves = [(g * 2 + c, (g ^ (turned(k) if c else k)) * 2 + c) for g in range(GROUP) for c in range(2)]
        received.append(lax.ppermute(partial[k], ("x", "y", "c"), moves))
    return received


def attention_kernel(ids_ref, *refs):
    own, near, far = refs[:3]
    pieces = refs[3:8]
    out_ref, q_s, k_s, v_s, level_s = refs[8:]
    group, z, core, w = ids_ref[0], ids_ref[1], ids_ref[2], ids_ref[3]
    x, y = group >> 2, group & 3
    first = 1 + 2 * core
    for rel_y, ref, base in ((0, own, 0), (first, near, 0), (4 - first, far, 0), (2, far, 2 * PIECE)):
        for rel_x in range(NX):
            rows = slice(base + rel_x * PIECE, base + (rel_x + 1) * PIECE)
            place = (x ^ rel_x) * NY + (y ^ rel_y)
            for head in range(4):
                q_s[head // 2, place, head % 2] = ref[rows, head * HD : (head + 1) * HD]
    places = z_order(core, z)
    index = 0
    for piece in pieces:
        for part in range(piece.shape[0] // PIECE):
            start = pl.multiple_of(places[index] * PIECE, PIECE)
            rows = slice(part * PIECE, (part + 1) * PIECE)
            for half in range(2):
                k_s[half, pl.ds(start, PIECE), :] = piece[rows, half * HD : (half + 1) * HD]
                v_s[half, pl.ds(start, PIECE), :] = piece[rows, (2 + half) * HD : (3 + half) * HD]
            index += 1
    level_s[...] = jnp.full((PIECE, HD), NEGATIVE, jnp.float32)

    keys = NZ * PIECE
    width = 4 * PIECE

    def slot(source):
        upper = source >> 2
        end_x = ((source >> 1) & 1) ^ w
        end_y = (((source & 1) ^ upper) << 1) | ((z & 1) ^ upper)
        return position(core, group ^ ((end_x << 2) | end_y))

    def one(half, pair, masked):
        query = q_s[half, pl.ds(pair * 2, 2)].reshape(width, HD)
        scores = lax.dot_general(query, k_s[half], NT, preferred_element_type=jnp.float32)
        if masked:
            row = lax.broadcasted_iota(jnp.int32, (width, 1), 0)
            source = pair * 2 + row // (2 * PIECE)
            at_z = ((z & 1) << 2) | ((z >> 1) ^ (3 * (source >> 2)))
            last = (source * NZ + at_z) * PIECE + row % PIECE - group * keys
            column = lax.broadcasted_iota(jnp.int32, (width, keys), 1)
            scores = jnp.where(column <= last, scores, NEGATIVE)
        highest = jnp.max(scores, axis=1, keepdims=True)
        weights = jnp.exp2(scores - highest)
        total = jnp.sum(weights, axis=1, keepdims=True)
        summed = jnp.dot(weights.astype(jnp.bfloat16), v_s[half], preferred_element_type=jnp.float32)
        normal = (summed / total).astype(jnp.bfloat16)
        level = highest + jnp.log2(total)
        lane = lax.broadcasted_iota(jnp.int32, (PIECE, HD), 1)
        for r in range(2):
            step = slot(pair * 2 + r)
            for j in range(2):
                base = (r * 2 + j) * PIECE
                head = half * 2 + j
                out_ref[step, :PIECE, head * HD : (head + 1) * HD] = normal[base : base + PIECE]
                level_s[...] = jnp.where(lane == step * 4 + head, level[base : base + PIECE], level_s[...])

    def body(pair, carry):
        full = pair * 2 > group
        none = pair * 2 + 1 < group

        @pl.when(full)
        def _():
            one(0, pair, False)
            one(1, pair, False)

        @pl.when(jnp.logical_not(jnp.logical_or(full, none)))
        def _():
            one(0, pair, True)
            one(1, pair, True)

        @pl.when(none)
        def _():
            for r in range(2):
                out_ref[slot(pair * 2 + r), :PIECE, :] = jnp.zeros((PIECE, 4 * HD), jnp.bfloat16)

        return carry

    lax.fori_loop(0, GROUP // 2, body, 0)
    levels = jnp.transpose(level_s[...])
    row = lax.broadcasted_iota(jnp.int32, (STATS, PIECE), 0)
    for step in range(GROUP):
        for head in range(4):
            line = jnp.broadcast_to(levels[step * 4 + head : step * 4 + head + 1], (STATS, PIECE))
            top = line.astype(jnp.bfloat16).astype(jnp.float32)
            middle = (line - top).astype(jnp.bfloat16).astype(jnp.float32)
            rest = line - top - middle
            stats = jnp.where(row == 0, top, jnp.where(row == 1, middle, jnp.where(row == 2, rest, 0.0)))
            out_ref[step, PIECE:, head * HD : (head + 1) * HD] = stats.astype(jnp.bfloat16)


def attention(ids, queries, pieces):
    flops = 2 * 2 * 4 * GROUP * PIECE * NZ * PIECE * HD
    return pl.pallas_call(
        attention_kernel,
        out_shape=jax.ShapeDtypeStruct((GROUP, PIECE + STATS, 4 * HD), jnp.bfloat16),
        in_specs=[SMEM] + [VMEM] * 8,
        out_specs=VMEM,
        scratch_shapes=[
            pltpu.VMEM((2, GROUP, 2, PIECE, HD), jnp.bfloat16),
            pltpu.VMEM((2, NZ * PIECE, HD), jnp.bfloat16),
            pltpu.VMEM((2, NZ * PIECE, HD), jnp.bfloat16),
            pltpu.VMEM((PIECE, HD), jnp.float32),
        ],
        compiler_params=pltpu.CompilerParams(vmem_limit_bytes=VMEM_LIMIT),
        cost_estimate=pl.CostEstimate(flops=flops, bytes_accessed=2**22, transcendentals=2**22),
    )(ids, *queries, *pieces)


def combine_kernel(ids_ref, partial, *refs):
    pieces = [partial.at[0]] + list(refs[: GROUP - 1])
    keep_out, give_out = refs[GROUP - 1 :]
    second_stays = (ids_ref[0] & 1) == 1
    stats = [piece[PIECE:, :].astype(jnp.float32) for piece in pieces]
    levels = [s[0:1] + s[1:2] + s[2:3] for s in stats]
    highest = functools.reduce(jnp.maximum, levels)
    shares = [jnp.exp2(level - highest) for level in levels]
    scale = 1.0 / functools.reduce(jnp.add, shares)
    table = jnp.concatenate([share * scale for share in shares], axis=0)
    for head in range(4):
        lanes = slice(head * HD, (head + 1) * HD)
        columns = jnp.transpose(table[:, lanes])
        totals = []
        for first in (0, BLOCK):
            rows = slice(first, first + BLOCK)
            total = None
            for s in range(GROUP):
                term = pieces[s][rows, lanes].astype(jnp.float32) * columns[rows, s : s + 1]
                total = term if total is None else total + term
            totals.append(total)
        keep_out[:, lanes] = jnp.where(second_stays, totals[1], totals[0]).astype(jnp.bfloat16)
        give_out[:, lanes] = jnp.where(second_stays, totals[0], totals[1]).astype(jnp.bfloat16)


def combine(ids, partial, received):
    block = jax.ShapeDtypeStruct((BLOCK, 4 * HD), jnp.bfloat16)
    return pl.pallas_call(
        combine_kernel,
        out_shape=(block, block),
        in_specs=[SMEM] + [VMEM] * GROUP,
        out_specs=(VMEM, VMEM),
        compiler_params=SMALL,
    )(ids, partial, *received)


TILE = 768


def project_kernel(ids_ref, kept, taken, weight, other_out, mine_out, rows_s):
    core = ids_ref[2]
    quarter = PIECE // 4
    kept_high = ((ids_ref[0] ^ ids_ref[1]) & 1) == 1
    first, second = kept[...], taken[...]
    low = jnp.where(kept_high, second, first)
    high = jnp.where(kept_high, first, second)
    for k, block in enumerate((low, high)):
        for part in range(2):
            own = 1 - (part ^ core)
            start = pl.multiple_of(own * BLOCK + k * quarter, quarter)
            rows_s[pl.ds(start, quarter), :] = block[part * quarter : (part + 1) * quarter]
    rows = rows_s[...]
    for tile in range(weight.shape[1] // TILE):
        lanes = slice(tile * TILE, (tile + 1) * TILE)
        product = jnp.dot(rows, weight[:, lanes], preferred_element_type=jnp.float32).astype(jnp.bfloat16)
        other_out[:, lanes] = product[:BLOCK]
        mine_out[:, lanes] = product[BLOCK:]


def project(ids, kept, taken, out_weight):
    half = jax.ShapeDtypeStruct((BLOCK, out_weight.shape[1]), jnp.bfloat16)
    return pl.pallas_call(
        project_kernel,
        out_shape=(half, half),
        in_specs=[SMEM] + [VMEM] * 3,
        out_specs=(VMEM, VMEM),
        scratch_shapes=[pltpu.VMEM((PIECE, 4 * HD), jnp.bfloat16)],
        compiler_params=pltpu.CompilerParams(vmem_limit_bytes=VMEM_LIMIT),
        cost_estimate=pl.CostEstimate(flops=2 * PIECE * 512 * 5376, bytes_accessed=2**23, transcendentals=0),
    )(ids, kept, taken, out_weight)


def on_device(queries, keys, values, positions, query_gain, key_gain, out_weight):
    x, y, z = lax.axis_index("x"), lax.axis_index("y"), lax.axis_index("z")
    w, c = lax.axis_index("w"), lax.axis_index("c")
    ids = jnp.stack([x * NY + y, z, c, w]).astype(jnp.int32)
    key_rows, cosines, sines = prepare_keys(keys, values, positions, key_gain)
    moved = lax.ppermute(prepare_queries(queries, cosines, sines, query_gain), ("x", "z"), move_pairs())
    pieces = gather_z(key_rows)
    partial = attention(ids, gather_xy(moved), pieces)
    kept, given = combine(ids, partial, exchange(partial))
    taken = lax.ppermute(given, "z", pairs(NZ, lambda i: i ^ 1))
    other, mine = project(ids, kept, taken, out_weight)
    got = lax.ppermute(other, "c", X_PAIRS)
    chip = (mine.astype(jnp.float32) + got.astype(jnp.float32)).reshape(2, PIECE // 4, -1)
    keep = lax.dynamic_index_in_dim(chip, w, 0, keepdims=False)
    give = lax.dynamic_index_in_dim(chip, 1 - w, 0, keepdims=False).astype(jnp.bfloat16)
    landed = lax.ppermute(give, ("x", "w"), pairs(4, lambda i: i ^ 3))
    return (keep + landed.astype(jnp.float32)).astype(jnp.bfloat16)


def solution(mesh):
    inner = Mesh(mesh.devices.reshape(NX, NY, NZ, 2, 2), ("x", "y", "z", "w", "c"))
    ctx, head = ("x", "y", "z"), ("w", "c")
    return jax.shard_map(
        on_device,
        mesh=inner,
        in_specs=(P(ctx, head), P(ctx, head), P(ctx, head), P(ctx), P(), P(), P(head, None)),
        out_specs=P(ctx + head, None),
        check_vma=False,
    )
```

```python
import functools

import jax
import jax.numpy as jnp
import numpy as np
from jax import lax
from jax.experimental import pallas as pl
from jax.experimental.pallas import tpu as pltpu
from jax.sharding import Mesh
from jax.sharding import PartitionSpec as P

EPSILON = 1e-06
HD = 128
PIECE = 128
NX, NY, NZ = 2, 4, 8
GROUP = NX * NY
QUERY_FACTOR = float(168.0**-0.5 / np.log(2.0))
NEGATIVE = -1e30
FREQUENCY = (1000000.0 ** (-2.0 * np.arange(64, dtype=np.float64) / 128)).astype(np.float32)
VMEM_LIMIT = 16 * 1024 * 1024
SMALL = pltpu.CompilerParams(vmem_limit_bytes=8 * 1024 * 1024)
NT = (((1,), (1,)), ((), ()))


def pairs(count, partner):
    return [(i, partner(i)) for i in range(count)]


def z_partner(which, z):
    return z ^ 1 if which == 0 else (((z + 1) ^ 1) + 7) & 7


def y_partner(which, y):
    return y ^ (1, 3)[which]


def by_core(count, partner):
    return tuple(
        [(i * 2 + core, partner(core ^ turn, i) * 2 + core) for i in range(count) for core in range(2)] for turn in range(2)
    )


Z_PAIRS = by_core(NZ, z_partner)
Y_PAIRS = by_core(NY, y_partner)
X_PAIRS = pairs(NX, lambda i: i ^ 1)
BLOCK = 64
STATS = 16
VMEM = pl.BlockSpec(memory_space=pltpu.VMEM)
SMEM = pl.BlockSpec(memory_space=pltpu.SMEM)


def rotate(vector, gain, cosines, sines):
    vector = vector.astype(jnp.float32)
    normed = vector * lax.rsqrt(jnp.mean(vector * vector, axis=-1, keepdims=True) + EPSILON) * gain
    return normed * cosines + pltpu.roll(normed, HD // 2, 1) * sines


def prepare_keys_kernel(k_ref, v_ref, pos_ref, freq_ref, gain_ref, out, cos_out, sin_out):
    lane = lax.broadcasted_iota(jnp.int32, (PIECE, HD), 1)
    spread = jnp.broadcast_to(pos_ref[...].astype(jnp.float32), (PIECE, HD))
    angles = jnp.transpose(spread) * freq_ref[...]
    cosines = jnp.cos(angles)
    sines = jnp.where(lane < HD // 2, -1.0, 1.0) * jnp.sin(angles)
    cos_out[...] = cosines
    sin_out[...] = sines
    for head in range(2):
        cols = slice(head * HD, (head + 1) * HD)
        rows = rotate(k_ref[:, cols], gain_ref[...], cosines, sines)
        out[:, cols] = rows.astype(jnp.bfloat16)
    out[:, 2 * HD :] = v_ref[...]


def prepare_keys(keys, values, positions, gain):
    freq = jnp.asarray(np.concatenate([FREQUENCY, FREQUENCY])[None, :])
    table = jax.ShapeDtypeStruct((PIECE, HD), jnp.float32)
    return pl.pallas_call(
        prepare_keys_kernel,
        out_shape=(jax.ShapeDtypeStruct((PIECE, 4 * HD), jnp.bfloat16), table, table),
        in_specs=[VMEM] * 5,
        out_specs=(VMEM,) * 3,
    )(keys, values, positions[None, :], freq, gain[None, :])


def prepare_queries_kernel(q_ref, cos_ref, sin_ref, gain_ref, out):
    for head in range(4):
        cols = slice(head * HD, (head + 1) * HD)
        rows = rotate(q_ref[:, cols], gain_ref[...], cos_ref[...], sin_ref[...])
        out[:, cols] = (rows * QUERY_FACTOR).astype(jnp.bfloat16)


def prepare_queries(queries, cosines, sines, gain):
    return pl.pallas_call(
        prepare_queries_kernel,
        out_shape=jax.ShapeDtypeStruct((PIECE, 4 * HD), jnp.bfloat16),
        in_specs=[VMEM] * 4,
        out_specs=VMEM,
    )(queries, cosines, sines, gain[None, :])


def gather_z(own):
    here, there = Z_PAIRS
    one = lax.ppermute(own, ("z", "c"), here)
    two = lax.ppermute(jnp.concatenate([own, one], axis=0), ("z", "c"), there)
    three = lax.ppermute(two, ("z", "c"), here)
    four = lax.ppermute(three, ("z", "c"), there)
    return [own, one, two, three, four]


def z_order(core, z):
    def step(which, place):
        return jnp.where(which == 0, z_partner(0, place), z_partner(1, place))

    def here(place):
        return step(core, place)

    def there(place):
        return step(1 - core, place)

    far, near = there(z), here(z)
    two = [far, here(far)]
    three = [there(near), here(there(near))]
    four = [there(here(far)), here(there(here(far)))]
    return [z, near] + two + three + four


def move_pairs():
    return [(x * NZ + z, x * NZ + ((((z & 3) ^ (3 * x)) << 1) | (z >> 2))) for x in range(NX) for z in range(NZ)]


def gather_xy(own):
    both = jnp.concatenate([own, lax.ppermute(own, "x", X_PAIRS)], axis=0)
    near = lax.ppermute(both, ("y", "c"), Y_PAIRS[0])
    far = lax.ppermute(jnp.concatenate([both, near], axis=0), ("y", "c"), Y_PAIRS[1])
    return both, near, far


def turned(step):
    return (4 * (step & 1)) ^ ((step >> 1) & 1) ^ (3 * ((step >> 2) & 1))


def position(core, step):
    back = (2 * (step & 1)) ^ (6 * ((step >> 1) & 1)) ^ ((step >> 2) & 1)
    return jnp.where(core == 0, step, back)


def exchange(partial):
    received = []
    for k in range(1, GROUP):
        moves = [(g * 2 + c, (g ^ (turned(k) if c else k)) * 2 + c) for g in range(GROUP) for c in range(2)]
        received.append(lax.ppermute(partial[k], ("x", "y", "c"), moves))
    return received


def attention_kernel(ids_ref, *refs):
    own, near, far = refs[:3]
    pieces = refs[3:8]
    out_ref, q_s, k_s, v_s, level_s = refs[8:]
    group, z, core, w = ids_ref[0], ids_ref[1], ids_ref[2], ids_ref[3]
    x, y = group >> 2, group & 3
    first = 1 + 2 * core
    for rel_y, ref, base in ((0, own, 0), (first, near, 0), (4 - first, far, 0), (2, far, 2 * PIECE)):
        for rel_x in range(NX):
            rows = slice(base + rel_x * PIECE, base + (rel_x + 1) * PIECE)
            place = (x ^ rel_x) * NY + (y ^ rel_y)
            for head in range(4):
                q_s[head // 2, place, head % 2] = ref[rows, head * HD : (head + 1) * HD]
    places = z_order(core, z)
    index = 0
    for piece in pieces:
        for part in range(piece.shape[0] // PIECE):
            start = pl.multiple_of(places[index] * PIECE, PIECE)
            rows = slice(part * PIECE, (part + 1) * PIECE)
            for half in range(2):
                k_s[half, pl.ds(start, PIECE), :] = piece[rows, half * HD : (half + 1) * HD]
                v_s[half, pl.ds(start, PIECE), :] = piece[rows, (2 + half) * HD : (3 + half) * HD]
            index += 1
    level_s[...] = jnp.full((PIECE, HD), NEGATIVE, jnp.float32)

    keys = NZ * PIECE
    width = 4 * PIECE

    def slot(source):
        upper = source >> 2
        end_x = ((source >> 1) & 1) ^ w
        end_y = (((source & 1) ^ upper) << 1) | ((z & 1) ^ upper)
        return position(core, group ^ ((end_x << 2) | end_y))

    def score(half, pair, masked):
        query = q_s[half, pl.ds(pair * 2, 2)].reshape(width, HD)
        scores = lax.dot_general(query, k_s[half], NT, preferred_element_type=jnp.float32)
        if masked:
            row = lax.broadcasted_iota(jnp.int32, (width, 1), 0)
            source = pair * 2 + row // (2 * PIECE)
            at_z = ((z & 1) << 2) | ((z >> 1) ^ (3 * (source >> 2)))
            last = (source * NZ + at_z) * PIECE + row % PIECE - group * keys
            column = lax.broadcasted_iota(jnp.int32, (width, keys), 1)
            scores = jnp.where(column <= last, scores, NEGATIVE)
        return scores

    def finish(half, pair, scores):
        highest = jnp.max(scores, axis=1, keepdims=True)
        weights = jnp.exp2(scores - highest)
        total = jnp.sum(weights, axis=1, keepdims=True)
        summed = jnp.dot(weights.astype(jnp.bfloat16), v_s[half], preferred_element_type=jnp.float32)
        normal = (summed / total).astype(jnp.bfloat16)
        level = highest + jnp.log2(total)
        lane = lax.broadcasted_iota(jnp.int32, (PIECE, HD), 1)
        for r in range(2):
            step = slot(pair * 2 + r)
            for j in range(2):
                base = (r * 2 + j) * PIECE
                head = half * 2 + j
                out_ref[step, :PIECE, head * HD : (head + 1) * HD] = normal[base : base + PIECE]
                level_s[...] = jnp.where(lane == step * 4 + head, level[base : base + PIECE], level_s[...])

    def run(tiles):
        scores = score(*tiles[0])
        for index, tile in enumerate(tiles):
            following = score(*tiles[index + 1]) if index + 1 < len(tiles) else None
            finish(tile[0], tile[1], scores)
            scores = following

    def body(pair, carry):
        full = pair * 2 > group
        none = pair * 2 + 1 < group

        @pl.when(full)
        def _():
            run([(0, pair, False), (1, pair, False)])

        @pl.when(jnp.logical_not(jnp.logical_or(full, none)))
        def _():
            run([(0, pair, True), (1, pair, True)])

        @pl.when(none)
        def _():
            for r in range(2):
                out_ref[slot(pair * 2 + r), :PIECE, :] = jnp.zeros((PIECE, 4 * HD), jnp.bfloat16)

        return carry

    @pl.when(group < 2)
    def _():
        run([(half, pair, pair == 0) for pair in range(GROUP // 2) for half in range(2)])

    @pl.when(group >= 2)
    def _():
        lax.fori_loop(0, GROUP // 2, body, 0)

    levels = jnp.transpose(level_s[...])
    row = lax.broadcasted_iota(jnp.int32, (STATS, PIECE), 0)
    for step in range(GROUP):
        for head in range(4):
            line = jnp.broadcast_to(levels[step * 4 + head : step * 4 + head + 1], (STATS, PIECE))
            top = line.astype(jnp.bfloat16).astype(jnp.float32)
            middle = (line - top).astype(jnp.bfloat16).astype(jnp.float32)
            rest = line - top - middle
            stats = jnp.where(row == 0, top, jnp.where(row == 1, middle, jnp.where(row == 2, rest, 0.0)))
            out_ref[step, PIECE:, head * HD : (head + 1) * HD] = stats.astype(jnp.bfloat16)


def attention(ids, queries, pieces):
    flops = 2 * 2 * 4 * GROUP * PIECE * NZ * PIECE * HD
    return pl.pallas_call(
        attention_kernel,
        out_shape=jax.ShapeDtypeStruct((GROUP, PIECE + STATS, 4 * HD), jnp.bfloat16),
        in_specs=[SMEM] + [VMEM] * 8,
        out_specs=VMEM,
        scratch_shapes=[
            pltpu.VMEM((2, GROUP, 2, PIECE, HD), jnp.bfloat16),
            pltpu.VMEM((2, NZ * PIECE, HD), jnp.bfloat16),
            pltpu.VMEM((2, NZ * PIECE, HD), jnp.bfloat16),
            pltpu.VMEM((PIECE, HD), jnp.float32),
        ],
        compiler_params=pltpu.CompilerParams(vmem_limit_bytes=36 * 1024 * 1024),
        cost_estimate=pl.CostEstimate(flops=flops, bytes_accessed=2**22, transcendentals=2**22),
    )(ids, *queries, *pieces)


def combine_kernel(ids_ref, partial, *refs):
    pieces = [partial.at[0]] + list(refs[: GROUP - 1])
    keep_out, give_out = refs[GROUP - 1 :]
    second_stays = (ids_ref[0] & 1) == 1
    stats = [piece[PIECE:, :].astype(jnp.float32) for piece in pieces]
    levels = [s[0:1] + s[1:2] + s[2:3] for s in stats]
    highest = functools.reduce(jnp.maximum, levels)
    shares = [jnp.exp2(level - highest) for level in levels]
    scale = 1.0 / functools.reduce(jnp.add, shares)
    table = jnp.concatenate([share * scale for share in shares], axis=0)
    for head in range(4):
        lanes = slice(head * HD, (head + 1) * HD)
        columns = jnp.transpose(table[:, lanes])
        totals = []
        for first in (0, BLOCK):
            rows = slice(first, first + BLOCK)
            total = None
            for s in range(GROUP):
                term = pieces[s][rows, lanes].astype(jnp.float32) * columns[rows, s : s + 1]
                total = term if total is None else total + term
            totals.append(total)
        keep_out[:, lanes] = jnp.where(second_stays, totals[1], totals[0]).astype(jnp.bfloat16)
        give_out[:, lanes] = jnp.where(second_stays, totals[0], totals[1]).astype(jnp.bfloat16)


def combine(ids, partial, received):
    block = jax.ShapeDtypeStruct((BLOCK, 4 * HD), jnp.bfloat16)
    return pl.pallas_call(
        combine_kernel,
        out_shape=(block, block),
        in_specs=[SMEM] + [VMEM] * GROUP,
        out_specs=(VMEM, VMEM),
        compiler_params=SMALL,
    )(ids, partial, *received)


TILE = 896


CHUNKS = 3


def project_kernel(ids_ref, kept, taken, weight, *refs):
    others, mines, rows_s = refs[:CHUNKS], refs[CHUNKS : 2 * CHUNKS], refs[-1]
    core = ids_ref[2]
    quarter = PIECE // 4
    kept_high = ((ids_ref[0] ^ ids_ref[1]) & 1) == 1
    first, second = kept[...], taken[...]
    low = jnp.where(kept_high, second, first)
    high = jnp.where(kept_high, first, second)
    for k, block in enumerate((low, high)):
        for part in range(2):
            own = 1 - (part ^ core)
            start = pl.multiple_of(own * BLOCK + k * quarter, quarter)
            rows_s[pl.ds(start, quarter), :] = block[part * quarter : (part + 1) * quarter]
    rows = rows_s[...]
    tiles = weight.shape[1] // CHUNKS // TILE
    for chunk in range(CHUNKS):
        for tile in range(tiles):
            lanes = slice(tile * TILE, (tile + 1) * TILE)
            start = (chunk * tiles + tile) * TILE
            product = jnp.dot(rows, weight[:, start : start + TILE], preferred_element_type=jnp.float32)
            product = product.astype(jnp.bfloat16)
            others[chunk][:, lanes] = product[:BLOCK]
            mines[chunk][:, lanes] = product[BLOCK:]


def project(ids, kept, taken, out_weight):
    half = jax.ShapeDtypeStruct((BLOCK, out_weight.shape[1] // CHUNKS), jnp.bfloat16)
    return pl.pallas_call(
        project_kernel,
        out_shape=(half,) * (2 * CHUNKS),
        in_specs=[SMEM] + [VMEM] * 3,
        out_specs=(VMEM,) * (2 * CHUNKS),
        scratch_shapes=[pltpu.VMEM((PIECE, 4 * HD), jnp.bfloat16)],
        compiler_params=pltpu.CompilerParams(vmem_limit_bytes=VMEM_LIMIT),
        cost_estimate=pl.CostEstimate(flops=2 * PIECE * 512 * 5376, bytes_accessed=2**23, transcendentals=0),
    )(ids, kept, taken, out_weight)


def on_device(queries, keys, values, positions, query_gain, key_gain, out_weight):
    x, y, z = lax.axis_index("x"), lax.axis_index("y"), lax.axis_index("z")
    w, c = lax.axis_index("w"), lax.axis_index("c")
    ids = jnp.stack([x * NY + y, z, c, w]).astype(jnp.int32)
    key_rows, cosines, sines = prepare_keys(keys, values, positions, key_gain)
    moved = lax.ppermute(prepare_queries(queries, cosines, sines, query_gain), ("x", "z"), move_pairs())
    pieces = gather_z(key_rows)
    partial = attention(ids, gather_xy(moved), pieces)
    kept, given = combine(ids, partial, exchange(partial))
    taken = lax.ppermute(given, "z", pairs(NZ, lambda i: i ^ 1))
    products = project(ids, kept, taken, out_weight)
    result = []
    for other, mine in zip(products[:CHUNKS], products[CHUNKS:]):
        got = lax.ppermute(other, "c", X_PAIRS)
        chip = (mine.astype(jnp.float32) + got.astype(jnp.float32)).reshape(2, PIECE // 4, -1)
        keep = lax.dynamic_index_in_dim(chip, w, 0, keepdims=False)
        give = lax.dynamic_index_in_dim(chip, 1 - w, 0, keepdims=False).astype(jnp.bfloat16)
        landed = lax.ppermute(give, ("x", "w"), pairs(4, lambda i: i ^ 3))
        result.append((keep + landed.astype(jnp.float32)).astype(jnp.bfloat16))
    return jnp.concatenate(result, axis=1)


def solution(mesh):
    inner = Mesh(mesh.devices.reshape(NX, NY, NZ, 2, 2), ("x", "y", "z", "w", "c"))
    ctx, head = ("x", "y", "z"), ("w", "c")
    return jax.shard_map(
        on_device,
        mesh=inner,
        in_specs=(P(ctx, head), P(ctx, head), P(ctx, head), P(ctx), P(), P(), P(head, None)),
        out_specs=P(ctx + head, None),
        check_vma=False,
    )
```

```python
import functools

import jax
import jax.numpy as jnp
import numpy as np
from jax import lax
from jax.experimental import pallas as pl
from jax.experimental.pallas import tpu as pltpu
from jax.sharding import Mesh
from jax.sharding import PartitionSpec as P

EPSILON = 1e-06
HD = 128
PIECE = 128
NX, NY, NZ = 2, 4, 8
GROUP = NX * NY
QUERY_FACTOR = float(168.0**-0.5 / np.log(2.0))
NEGATIVE = -1e30
FREQUENCY = (1000000.0 ** (-2.0 * np.arange(64, dtype=np.float64) / 128)).astype(np.float32)
VMEM_LIMIT = 16 * 1024 * 1024
SMALL = pltpu.CompilerParams(vmem_limit_bytes=8 * 1024 * 1024)
NT = (((1,), (1,)), ((), ()))


def pairs(count, partner):
    return [(i, partner(i)) for i in range(count)]


def z_partner(which, z):
    return z ^ 1 if which == 0 else (((z + 1) ^ 1) + 7) & 7


def y_partner(which, y):
    return y ^ (1, 3)[which]


def by_core(count, partner):
    return tuple(
        [(i * 2 + core, partner(core ^ turn, i) * 2 + core) for i in range(count) for core in range(2)] for turn in range(2)
    )


Z_PAIRS = by_core(NZ, z_partner)
Y_PAIRS = by_core(NY, y_partner)
X_PAIRS = pairs(NX, lambda i: i ^ 1)
BLOCK = 64
STATS = 16
VMEM = pl.BlockSpec(memory_space=pltpu.VMEM)
SMEM = pl.BlockSpec(memory_space=pltpu.SMEM)


def rotate(vector, gain, cosines, sines):
    vector = vector.astype(jnp.float32)
    normed = vector * lax.rsqrt(jnp.mean(vector * vector, axis=-1, keepdims=True) + EPSILON) * gain
    return normed * cosines + pltpu.roll(normed, HD // 2, 1) * sines


def prepare_kernel(q_ref, k_ref, v_ref, pos_ref, freq_ref, q_gain, k_gain, q_out, kv_out):
    lane = lax.broadcasted_iota(jnp.int32, (PIECE, HD), 1)
    spread = jnp.broadcast_to(pos_ref[...].astype(jnp.float32), (PIECE, HD))
    angles = jnp.transpose(spread) * freq_ref[...]
    cosines = jnp.cos(angles)
    sines = jnp.where(lane < HD // 2, -1.0, 1.0) * jnp.sin(angles)
    for head in range(4):
        cols = slice(head * HD, (head + 1) * HD)
        rows = rotate(q_ref[:, cols], q_gain[...], cosines, sines)
        q_out[:, cols] = (rows * QUERY_FACTOR).astype(jnp.bfloat16)
    for head in range(2):
        cols = slice(head * HD, (head + 1) * HD)
        rows = rotate(k_ref[:, cols], k_gain[...], cosines, sines)
        kv_out[:, cols] = rows.astype(jnp.bfloat16)
    kv_out[:, 2 * HD :] = v_ref[...]


def prepare(queries, keys, values, positions, query_gain, key_gain):
    freq = jnp.asarray(np.concatenate([FREQUENCY, FREQUENCY])[None, :])
    piece = jax.ShapeDtypeStruct((PIECE, 4 * HD), jnp.bfloat16)
    return pl.pallas_call(
        prepare_kernel,
        out_shape=(piece, piece),
        in_specs=[VMEM] * 7,
        out_specs=(VMEM,) * 2,
    )(queries, keys, values, positions[None, :], freq, query_gain[None, :], key_gain[None, :])


def gather_z(own):
    here, there = Z_PAIRS
    one = lax.ppermute(own, ("z", "c"), here)
    two = lax.ppermute(jnp.concatenate([own, one], axis=0), ("z", "c"), there)
    three = lax.ppermute(two, ("z", "c"), here)
    four = lax.ppermute(three, ("z", "c"), there)
    return [own, one, two, three, four]


def z_order(core, z):
    def step(which, place):
        return jnp.where(which == 0, z_partner(0, place), z_partner(1, place))

    def here(place):
        return step(core, place)

    def there(place):
        return step(1 - core, place)

    far, near = there(z), here(z)
    two = [far, here(far)]
    three = [there(near), here(there(near))]
    four = [there(here(far)), here(there(here(far)))]
    return [z, near] + two + three + four


def move_pairs():
    return [(x * NZ + z, x * NZ + ((((z & 3) ^ (3 * x)) << 1) | (z >> 2))) for x in range(NX) for z in range(NZ)]


def gather_xy(own):
    both = jnp.concatenate([own, lax.ppermute(own, "x", X_PAIRS)], axis=0)
    near = lax.ppermute(both, ("y", "c"), Y_PAIRS[0])
    far = lax.ppermute(jnp.concatenate([both, near], axis=0), ("y", "c"), Y_PAIRS[1])
    return both, near, far


def turned(step):
    return (4 * (step & 1)) ^ ((step >> 1) & 1) ^ (3 * ((step >> 2) & 1))


def position(core, step):
    back = (2 * (step & 1)) ^ (6 * ((step >> 1) & 1)) ^ ((step >> 2) & 1)
    return jnp.where(core == 0, step, back)


def exchange(partial):
    received = []
    for k in range(1, GROUP):
        moves = [(g * 2 + c, (g ^ (turned(k) if c else k)) * 2 + c) for g in range(GROUP) for c in range(2)]
        received.append(lax.ppermute(partial[k], ("x", "y", "c"), moves))
    return received


def attention_kernel(ids_ref, *refs):
    own, near, far = refs[:3]
    pieces = refs[3:8]
    out_ref, q_s, k_s, v_s, level_s = refs[8:]
    group, z, core, w = ids_ref[0], ids_ref[1], ids_ref[2], ids_ref[3]
    x, y = group >> 2, group & 3
    first = 1 + 2 * core
    for rel_y, ref, base in ((0, own, 0), (first, near, 0), (4 - first, far, 0), (2, far, 2 * PIECE)):
        for rel_x in range(NX):
            rows = slice(base + rel_x * PIECE, base + (rel_x + 1) * PIECE)
            place = (x ^ rel_x) * NY + (y ^ rel_y)
            for head in range(4):
                q_s[head // 2, place, head % 2] = ref[rows, head * HD : (head + 1) * HD]
    places = z_order(core, z)
    index = 0
    for piece in pieces:
        for part in range(piece.shape[0] // PIECE):
            start = pl.multiple_of(places[index] * PIECE, PIECE)
            rows = slice(part * PIECE, (part + 1) * PIECE)
            for half in range(2):
                k_s[half, pl.ds(start, PIECE), :] = piece[rows, half * HD : (half + 1) * HD]
                v_s[half, pl.ds(start, PIECE), :] = piece[rows, (2 + half) * HD : (3 + half) * HD]
            index += 1
    level_s[...] = jnp.full((PIECE, HD), NEGATIVE, jnp.float32)

    keys = NZ * PIECE
    width = 4 * PIECE

    def slot(source):
        upper = source >> 2
        end_x = ((source >> 1) & 1) ^ w
        end_y = (((source & 1) ^ upper) << 1) | ((z & 1) ^ upper)
        return position(core, group ^ ((end_x << 2) | end_y))

    def score(half, pair, masked):
        query = q_s[half, pl.ds(pair * 2, 2)].reshape(width, HD)
        scores = lax.dot_general(query, k_s[half], NT, preferred_element_type=jnp.float32)
        if masked:
            row = lax.broadcasted_iota(jnp.int32, (width, 1), 0)
            source = pair * 2 + row // (2 * PIECE)
            at_z = ((z & 1) << 2) | ((z >> 1) ^ (3 * (source >> 2)))
            last = (source * NZ + at_z) * PIECE + row % PIECE - group * keys
            column = lax.broadcasted_iota(jnp.int32, (width, keys), 1)
            scores = jnp.where(column <= last, scores, NEGATIVE)
        return scores

    def finish(half, pair, scores):
        highest = jnp.max(scores, axis=1, keepdims=True)
        weights = jnp.exp2(scores - highest)
        total = jnp.sum(weights, axis=1, keepdims=True)
        summed = jnp.dot(weights.astype(jnp.bfloat16), v_s[half], preferred_element_type=jnp.float32)
        normal = (summed / total).astype(jnp.bfloat16)
        level = highest + jnp.log2(total)
        lane = lax.broadcasted_iota(jnp.int32, (PIECE, HD), 1)
        for r in range(2):
            step = slot(pair * 2 + r)
            for j in range(2):
                base = (r * 2 + j) * PIECE
                head = half * 2 + j
                out_ref[step, :PIECE, head * HD : (head + 1) * HD] = normal[base : base + PIECE]
                level_s[...] = jnp.where(lane == step * 4 + head, level[base : base + PIECE], level_s[...])

    def run(tiles):
        scores = score(*tiles[0])
        for index, tile in enumerate(tiles):
            following = score(*tiles[index + 1]) if index + 1 < len(tiles) else None
            finish(tile[0], tile[1], scores)
            scores = following

    def body(pair, carry):
        full = pair * 2 > group
        none = pair * 2 + 1 < group

        @pl.when(full)
        def _():
            run([(0, pair, False), (1, pair, False)])

        @pl.when(jnp.logical_not(jnp.logical_or(full, none)))
        def _():
            run([(0, pair, True), (1, pair, True)])

        @pl.when(none)
        def _():
            for r in range(2):
                out_ref[slot(pair * 2 + r), :PIECE, :] = jnp.zeros((PIECE, 4 * HD), jnp.bfloat16)

        return carry

    @pl.when(group < 2)
    def _():
        run([(half, pair, pair == 0) for pair in range(GROUP // 2) for half in range(2)])

    @pl.when(group >= 2)
    def _():
        lax.fori_loop(0, GROUP // 2, body, 0)

    levels = jnp.transpose(level_s[...])
    row = lax.broadcasted_iota(jnp.int32, (STATS, PIECE), 0)
    for step in range(GROUP):
        for head in range(4):
            line = jnp.broadcast_to(levels[step * 4 + head : step * 4 + head + 1], (STATS, PIECE))
            top = line.astype(jnp.bfloat16).astype(jnp.float32)
            middle = (line - top).astype(jnp.bfloat16).astype(jnp.float32)
            rest = line - top - middle
            stats = jnp.where(row == 0, top, jnp.where(row == 1, middle, jnp.where(row == 2, rest, 0.0)))
            out_ref[step, PIECE:, head * HD : (head + 1) * HD] = stats.astype(jnp.bfloat16)


def attention(ids, queries, pieces):
    flops = 2 * 2 * 4 * GROUP * PIECE * NZ * PIECE * HD
    return pl.pallas_call(
        attention_kernel,
        out_shape=jax.ShapeDtypeStruct((GROUP, PIECE + STATS, 4 * HD), jnp.bfloat16),
        in_specs=[SMEM] + [VMEM] * 8,
        out_specs=VMEM,
        scratch_shapes=[
            pltpu.VMEM((2, GROUP, 2, PIECE, HD), jnp.bfloat16),
            pltpu.VMEM((2, NZ * PIECE, HD), jnp.bfloat16),
            pltpu.VMEM((2, NZ * PIECE, HD), jnp.bfloat16),
            pltpu.VMEM((PIECE, HD), jnp.float32),
        ],
        compiler_params=pltpu.CompilerParams(vmem_limit_bytes=36 * 1024 * 1024),
        cost_estimate=pl.CostEstimate(flops=flops, bytes_accessed=2**22, transcendentals=2**22),
    )(ids, *queries, *pieces)


def combine_kernel(ids_ref, partial, *refs):
    pieces = [partial.at[0]] + list(refs[: GROUP - 1])
    keep_out, give_out = refs[GROUP - 1 :]
    second_stays = (ids_ref[0] & 1) == 1
    stats = [piece[PIECE:, :].astype(jnp.float32) for piece in pieces]
    levels = [s[0:1] + s[1:2] + s[2:3] for s in stats]
    highest = functools.reduce(jnp.maximum, levels)
    shares = [jnp.exp2(level - highest) for level in levels]
    scale = 1.0 / functools.reduce(jnp.add, shares)
    table = jnp.concatenate([share * scale for share in shares], axis=0)
    for head in range(4):
        lanes = slice(head * HD, (head + 1) * HD)
        columns = jnp.transpose(table[:, lanes])
        totals = []
        for first in (0, BLOCK):
            rows = slice(first, first + BLOCK)
            total = None
            for s in range(GROUP):
                term = pieces[s][rows, lanes].astype(jnp.float32) * columns[rows, s : s + 1]
                total = term if total is None else total + term
            totals.append(total)
        keep_out[:, lanes] = jnp.where(second_stays, totals[1], totals[0]).astype(jnp.bfloat16)
        give_out[:, lanes] = jnp.where(second_stays, totals[0], totals[1]).astype(jnp.bfloat16)


def combine(ids, partial, received):
    block = jax.ShapeDtypeStruct((BLOCK, 4 * HD), jnp.bfloat16)
    return pl.pallas_call(
        combine_kernel,
        out_shape=(block, block),
        in_specs=[SMEM] + [VMEM] * GROUP,
        out_specs=(VMEM, VMEM),
        compiler_params=SMALL,
    )(ids, partial, *received)


TILE = 896


CHUNKS = 3


def project_kernel(ids_ref, kept, taken, weight, *refs):
    others, mines, rows_s = refs[:CHUNKS], refs[CHUNKS : 2 * CHUNKS], refs[-1]
    core = ids_ref[2]
    quarter = PIECE // 4
    kept_high = ((ids_ref[0] ^ ids_ref[1]) & 1) == 1
    first, second = kept[...], taken[...]
    low = jnp.where(kept_high, second, first)
    high = jnp.where(kept_high, first, second)
    for k, block in enumerate((low, high)):
        for part in range(2):
            own = 1 - (part ^ core)
            start = pl.multiple_of(own * BLOCK + k * quarter, quarter)
            rows_s[pl.ds(start, quarter), :] = block[part * quarter : (part + 1) * quarter]
    rows = rows_s[...]
    tiles = weight.shape[1] // CHUNKS // TILE
    for chunk in range(CHUNKS):
        for tile in range(tiles):
            lanes = slice(tile * TILE, (tile + 1) * TILE)
            start = (chunk * tiles + tile) * TILE
            product = jnp.dot(rows, weight[:, start : start + TILE], preferred_element_type=jnp.float32)
            product = product.astype(jnp.bfloat16)
            others[chunk][:, lanes] = product[:BLOCK]
            mines[chunk][:, lanes] = product[BLOCK:]


def project(ids, kept, taken, out_weight):
    half = jax.ShapeDtypeStruct((BLOCK, out_weight.shape[1] // CHUNKS), jnp.bfloat16)
    return pl.pallas_call(
        project_kernel,
        out_shape=(half,) * (2 * CHUNKS),
        in_specs=[SMEM] + [VMEM] * 3,
        out_specs=(VMEM,) * (2 * CHUNKS),
        scratch_shapes=[pltpu.VMEM((PIECE, 4 * HD), jnp.bfloat16)],
        compiler_params=pltpu.CompilerParams(vmem_limit_bytes=VMEM_LIMIT),
        cost_estimate=pl.CostEstimate(flops=2 * PIECE * 512 * 5376, bytes_accessed=2**23, transcendentals=0),
    )(ids, kept, taken, out_weight)


def on_device(queries, keys, values, positions, query_gain, key_gain, out_weight):
    x, y, z = lax.axis_index("x"), lax.axis_index("y"), lax.axis_index("z")
    w, c = lax.axis_index("w"), lax.axis_index("c")
    ids = jnp.stack([x * NY + y, z, c, w]).astype(jnp.int32)
    query_rows, key_rows = prepare(queries, keys, values, positions, query_gain, key_gain)
    moved = lax.ppermute(query_rows, ("x", "z"), move_pairs())
    pieces = gather_z(key_rows)
    partial = attention(ids, gather_xy(moved), pieces)
    kept, given = combine(ids, partial, exchange(partial))
    taken = lax.ppermute(given, "z", pairs(NZ, lambda i: i ^ 1))
    products = project(ids, kept, taken, out_weight)
    result = []
    for other, mine in zip(products[:CHUNKS], products[CHUNKS:]):
        got = lax.ppermute(other, "c", X_PAIRS)
        chip = (mine.astype(jnp.float32) + got.astype(jnp.float32)).reshape(2, PIECE // 4, -1)
        keep = lax.dynamic_index_in_dim(chip, w, 0, keepdims=False)
        give = lax.dynamic_index_in_dim(chip, 1 - w, 0, keepdims=False).astype(jnp.bfloat16)
        landed = lax.ppermute(give, ("x", "w"), pairs(4, lambda i: i ^ 3))
        result.append((keep + landed.astype(jnp.float32)).astype(jnp.bfloat16))
    return jnp.concatenate(result, axis=1)


def solution(mesh):
    inner = Mesh(mesh.devices.reshape(NX, NY, NZ, 2, 2), ("x", "y", "z", "w", "c"))
    ctx, head = ("x", "y", "z"), ("w", "c")
    return jax.shard_map(
        on_device,
        mesh=inner,
        in_specs=(P(ctx, head), P(ctx, head), P(ctx, head), P(ctx), P(), P(), P(head, None)),
        out_specs=P(ctx + head, None),
        check_vma=False,
    )
```

```python
import functools

import jax
import jax.numpy as jnp
import numpy as np
from jax import lax
from jax.experimental import pallas as pl
from jax.experimental.pallas import tpu as pltpu
from jax.sharding import Mesh
from jax.sharding import PartitionSpec as P

EPSILON = 1e-06
HD = 128
PIECE = 128
NX, NY, NZ = 2, 4, 8
GROUP = NX * NY
QUERY_FACTOR = float(168.0**-0.5 / np.log(2.0))
NEGATIVE = -1e30
FREQUENCY = (1000000.0 ** (-2.0 * np.arange(64, dtype=np.float64) / 128)).astype(np.float32)
VMEM_LIMIT = 16 * 1024 * 1024
SMALL = pltpu.CompilerParams(vmem_limit_bytes=8 * 1024 * 1024)
NT = (((1,), (1,)), ((), ()))


def pairs(count, partner):
    return [(i, partner(i)) for i in range(count)]


def z_partner(which, z):
    return z ^ 1 if which == 0 else (((z + 1) ^ 1) + 7) & 7


def y_partner(which, y):
    return y ^ (1, 3)[which]


def by_core(count, partner):
    return tuple(
        [(i * 2 + core, partner(core ^ turn, i) * 2 + core) for i in range(count) for core in range(2)] for turn in range(2)
    )


Z_PAIRS = by_core(NZ, z_partner)
Y_PAIRS = by_core(NY, y_partner)
X_PAIRS = pairs(NX, lambda i: i ^ 1)
BLOCK = 64
STATS = 16
VMEM = pl.BlockSpec(memory_space=pltpu.VMEM)
SMEM = pl.BlockSpec(memory_space=pltpu.SMEM)


def rotate(vector, gain, cosines, sines):
    vector = vector.astype(jnp.float32)
    normed = vector * lax.rsqrt(jnp.mean(vector * vector, axis=-1, keepdims=True) + EPSILON) * gain
    return normed * cosines + pltpu.roll(normed, HD // 2, 1) * sines


def prepare_kernel(q_ref, k_ref, v_ref, pos_ref, freq_ref, q_gain, k_gain, q_out, kv_out):
    lane = lax.broadcasted_iota(jnp.int32, (PIECE, HD), 1)
    spread = jnp.broadcast_to(pos_ref[...].astype(jnp.float32), (PIECE, HD))
    angles = jnp.transpose(spread) * freq_ref[...]
    cosines = jnp.cos(angles)
    sines = jnp.where(lane < HD // 2, -1.0, 1.0) * jnp.sin(angles)
    for head in range(4):
        cols = slice(head * HD, (head + 1) * HD)
        rows = rotate(q_ref[:, cols], q_gain[...], cosines, sines)
        q_out[:, cols] = (rows * QUERY_FACTOR).astype(jnp.bfloat16)
    for head in range(2):
        cols = slice(head * HD, (head + 1) * HD)
        rows = rotate(k_ref[:, cols], k_gain[...], cosines, sines)
        kv_out[:, cols] = rows.astype(jnp.bfloat16)
    kv_out[:, 2 * HD :] = v_ref[...]


def prepare(queries, keys, values, positions, query_gain, key_gain):
    freq = jnp.asarray(np.concatenate([FREQUENCY, FREQUENCY])[None, :])
    piece = jax.ShapeDtypeStruct((PIECE, 4 * HD), jnp.bfloat16)
    return pl.pallas_call(
        prepare_kernel,
        out_shape=(piece, piece),
        in_specs=[VMEM] * 7,
        out_specs=(VMEM,) * 2,
    )(queries, keys, values, positions[None, :], freq, query_gain[None, :], key_gain[None, :])


def gather_z(own):
    here, there = Z_PAIRS
    one = lax.ppermute(own, ("z", "c"), here)
    two = lax.ppermute(jnp.concatenate([own, one], axis=0), ("z", "c"), there)
    three = lax.ppermute(two, ("z", "c"), here)
    four = lax.ppermute(three, ("z", "c"), there)
    return [own, one, two, three, four]


def z_order(core, z):
    def step(which, place):
        return jnp.where(which == 0, z_partner(0, place), z_partner(1, place))

    def here(place):
        return step(core, place)

    def there(place):
        return step(1 - core, place)

    far, near = there(z), here(z)
    two = [far, here(far)]
    three = [there(near), here(there(near))]
    four = [there(here(far)), here(there(here(far)))]
    return [z, near] + two + three + four


def move_pairs():
    return [(x * NZ + z, x * NZ + ((((z & 3) ^ (3 * x)) << 1) | (z >> 2))) for x in range(NX) for z in range(NZ)]


def gather_xy(own):
    both = jnp.concatenate([own, lax.ppermute(own, "x", X_PAIRS)], axis=0)
    near = lax.ppermute(both, ("y", "c"), Y_PAIRS[0])
    far = lax.ppermute(jnp.concatenate([both, near], axis=0), ("y", "c"), Y_PAIRS[1])
    return both, near, far


def exchange(partial):
    return [
        lax.ppermute(partial[step], ("x", "y"), pairs(GROUP, lambda i: i ^ step)) for step in range(1, GROUP)
    ]


def attention_kernel(ids_ref, *refs):
    own, near, far = refs[:3]
    pieces = refs[3:8]
    out_ref, q_s, k_s, v_s, level_s = refs[8:]
    group, z, core, w = ids_ref[0], ids_ref[1], ids_ref[2], ids_ref[3]
    x, y = group >> 2, group & 3
    first = 1 + 2 * core
    for rel_y, ref, base in ((0, own, 0), (first, near, 0), (4 - first, far, 0), (2, far, 2 * PIECE)):
        for rel_x in range(NX):
            rows = slice(base + rel_x * PIECE, base + (rel_x + 1) * PIECE)
            place = (x ^ rel_x) * NY + (y ^ rel_y)
            for head in range(4):
                q_s[head // 2, place, head % 2] = ref[rows, head * HD : (head + 1) * HD]
    places = z_order(core, z)
    index = 0
    for piece in pieces:
        for part in range(piece.shape[0] // PIECE):
            start = pl.multiple_of(places[index] * PIECE, PIECE)
            rows = slice(part * PIECE, (part + 1) * PIECE)
            for half in range(2):
                k_s[half, pl.ds(start, PIECE), :] = piece[rows, half * HD : (half + 1) * HD]
                v_s[half, pl.ds(start, PIECE), :] = piece[rows, (2 + half) * HD : (3 + half) * HD]
            index += 1
    level_s[...] = jnp.full((PIECE, HD), NEGATIVE, jnp.float32)

    keys = NZ * PIECE
    width = 4 * PIECE

    def slot(source):
        upper = source >> 2
        end_x = ((source >> 1) & 1) ^ w
        end_y = (((source & 1) ^ upper) << 1) | ((z & 1) ^ upper)
        return group ^ ((end_x << 2) | end_y)

    def score(half, pair, masked):
        query = q_s[half, pl.ds(pair * 2, 2)].reshape(width, HD)
        scores = lax.dot_general(query, k_s[half], NT, preferred_element_type=jnp.float32)
        if masked:
            row = lax.broadcasted_iota(jnp.int32, (width, 1), 0)
            source = pair * 2 + row // (2 * PIECE)
            at_z = ((z & 1) << 2) | ((z >> 1) ^ (3 * (source >> 2)))
            last = (source * NZ + at_z) * PIECE + row % PIECE - group * keys
            column = lax.broadcasted_iota(jnp.int32, (width, keys), 1)
            scores = jnp.where(column <= last, scores, NEGATIVE)
        return scores

    def finish(half, pair, scores):
        highest = jnp.max(scores, axis=1, keepdims=True)
        weights = jnp.exp2(scores - highest)
        total = jnp.sum(weights, axis=1, keepdims=True)
        summed = jnp.dot(weights.astype(jnp.bfloat16), v_s[half], preferred_element_type=jnp.float32)
        normal = (summed / total).astype(jnp.bfloat16)
        level = highest + jnp.log2(total)
        lane = lax.broadcasted_iota(jnp.int32, (PIECE, HD), 1)
        for r in range(2):
            step = slot(pair * 2 + r)
            for j in range(2):
                base = (r * 2 + j) * PIECE
                head = half * 2 + j
                out_ref[step, :PIECE, head * HD : (head + 1) * HD] = normal[base : base + PIECE]
                level_s[...] = jnp.where(lane == step * 4 + head, level[base : base + PIECE], level_s[...])

    def run(tiles):
        scores = score(*tiles[0])
        for index, tile in enumerate(tiles):
            following = score(*tiles[index + 1]) if index + 1 < len(tiles) else None
            finish(tile[0], tile[1], scores)
            scores = following

    def body(pair, carry):
        full = pair * 2 > group
        none = pair * 2 + 1 < group

        @pl.when(full)
        def _():
            run([(0, pair, False), (1, pair, False)])

        @pl.when(jnp.logical_not(jnp.logical_or(full, none)))
        def _():
            run([(0, pair, True), (1, pair, True)])

        @pl.when(none)
        def _():
            for r in range(2):
                out_ref[slot(pair * 2 + r), :PIECE, :] = jnp.zeros((PIECE, 4 * HD), jnp.bfloat16)

        return carry

    @pl.when(group < 2)
    def _():
        run([(half, pair, pair == 0) for pair in range(GROUP // 2) for half in range(2)])

    @pl.when(group >= 2)
    def _():
        lax.fori_loop(0, GROUP // 2, body, 0)

    levels = jnp.transpose(level_s[...])
    row = lax.broadcasted_iota(jnp.int32, (STATS, PIECE), 0)
    for step in range(GROUP):
        for head in range(4):
            line = jnp.broadcast_to(levels[step * 4 + head : step * 4 + head + 1], (STATS, PIECE))
            top = line.astype(jnp.bfloat16).astype(jnp.float32)
            middle = (line - top).astype(jnp.bfloat16).astype(jnp.float32)
            rest = line - top - middle
            stats = jnp.where(row == 0, top, jnp.where(row == 1, middle, jnp.where(row == 2, rest, 0.0)))
            out_ref[step, PIECE:, head * HD : (head + 1) * HD] = stats.astype(jnp.bfloat16)


def attention(ids, queries, pieces):
    flops = 2 * 2 * 4 * GROUP * PIECE * NZ * PIECE * HD
    return pl.pallas_call(
        attention_kernel,
        out_shape=jax.ShapeDtypeStruct((GROUP, PIECE + STATS, 4 * HD), jnp.bfloat16),
        in_specs=[SMEM] + [VMEM] * 8,
        out_specs=VMEM,
        scratch_shapes=[
            pltpu.VMEM((2, GROUP, 2, PIECE, HD), jnp.bfloat16),
            pltpu.VMEM((2, NZ * PIECE, HD), jnp.bfloat16),
            pltpu.VMEM((2, NZ * PIECE, HD), jnp.bfloat16),
            pltpu.VMEM((PIECE, HD), jnp.float32),
        ],
        compiler_params=pltpu.CompilerParams(vmem_limit_bytes=36 * 1024 * 1024),
        cost_estimate=pl.CostEstimate(flops=flops, bytes_accessed=2**22, transcendentals=2**22),
    )(ids, *queries, *pieces)


def combine_kernel(ids_ref, partial, *refs):
    pieces = [partial.at[0]] + list(refs[: GROUP - 1])
    keep_out, give_out = refs[GROUP - 1 :]
    second_stays = (ids_ref[0] & 1) == 1
    stats = [piece[PIECE:, :].astype(jnp.float32) for piece in pieces]
    levels = [s[0:1] + s[1:2] + s[2:3] for s in stats]
    highest = functools.reduce(jnp.maximum, levels)
    shares = [jnp.exp2(level - highest) for level in levels]
    scale = 1.0 / functools.reduce(jnp.add, shares)
    table = jnp.concatenate([share * scale for share in shares], axis=0)
    for head in range(4):
        lanes = slice(head * HD, (head + 1) * HD)
        columns = jnp.transpose(table[:, lanes])
        totals = []
        for first in (0, BLOCK):
            rows = slice(first, first + BLOCK)
            total = None
            for s in range(GROUP):
                term = pieces[s][rows, lanes].astype(jnp.float32) * columns[rows, s : s + 1]
                total = term if total is None else total + term
            totals.append(total)
        keep_out[:, lanes] = jnp.where(second_stays, totals[1], totals[0]).astype(jnp.bfloat16)
        give_out[:, lanes] = jnp.where(second_stays, totals[0], totals[1]).astype(jnp.bfloat16)


def combine(ids, partial, received):
    block = jax.ShapeDtypeStruct((BLOCK, 4 * HD), jnp.bfloat16)
    return pl.pallas_call(
        combine_kernel,
        out_shape=(block, block),
        in_specs=[SMEM] + [VMEM] * GROUP,
        out_specs=(VMEM, VMEM),
        compiler_params=SMALL,
    )(ids, partial, *received)


TILE = 896


CHUNKS = 3


def project_kernel(ids_ref, kept, taken, weight, *refs):
    others, mines, rows_s = refs[:CHUNKS], refs[CHUNKS : 2 * CHUNKS], refs[-1]
    core = ids_ref[2]
    quarter = PIECE // 4
    kept_high = ((ids_ref[0] ^ ids_ref[1]) & 1) == 1
    first, second = kept[...], taken[...]
    low = jnp.where(kept_high, second, first)
    high = jnp.where(kept_high, first, second)
    for k, block in enumerate((low, high)):
        for part in range(2):
            own = 1 - (part ^ core)
            start = pl.multiple_of(own * BLOCK + k * quarter, quarter)
            rows_s[pl.ds(start, quarter), :] = block[part * quarter : (part + 1) * quarter]
    rows = rows_s[...]
    tiles = weight.shape[1] // CHUNKS // TILE
    for chunk in range(CHUNKS):
        for tile in range(tiles):
            lanes = slice(tile * TILE, (tile + 1) * TILE)
            start = (chunk * tiles + tile) * TILE
            product = jnp.dot(rows, weight[:, start : start + TILE], preferred_element_type=jnp.float32)
            product = product.astype(jnp.bfloat16)
            others[chunk][:, lanes] = product[:BLOCK]
            mines[chunk][:, lanes] = product[BLOCK:]


def project(ids, kept, taken, out_weight):
    half = jax.ShapeDtypeStruct((BLOCK, out_weight.shape[1] // CHUNKS), jnp.bfloat16)
    return pl.pallas_call(
        project_kernel,
        out_shape=(half,) * (2 * CHUNKS),
        in_specs=[SMEM] + [VMEM] * 3,
        out_specs=(VMEM,) * (2 * CHUNKS),
        scratch_shapes=[pltpu.VMEM((PIECE, 4 * HD), jnp.bfloat16)],
        compiler_params=pltpu.CompilerParams(vmem_limit_bytes=VMEM_LIMIT),
        cost_estimate=pl.CostEstimate(flops=2 * PIECE * 512 * 5376, bytes_accessed=2**23, transcendentals=0),
    )(ids, kept, taken, out_weight)


def on_device(queries, keys, values, positions, query_gain, key_gain, out_weight):
    x, y, z = lax.axis_index("x"), lax.axis_index("y"), lax.axis_index("z")
    w, c = lax.axis_index("w"), lax.axis_index("c")
    ids = jnp.stack([x * NY + y, z, c, w]).astype(jnp.int32)
    query_rows, key_rows = prepare(queries, keys, values, positions, query_gain, key_gain)
    moved = lax.ppermute(query_rows, ("x", "z"), move_pairs())
    pieces = gather_z(key_rows)
    partial = attention(ids, gather_xy(moved), pieces)
    kept, given = combine(ids, partial, exchange(partial))
    taken = lax.ppermute(given, "z", pairs(NZ, lambda i: i ^ 1))
    products = project(ids, kept, taken, out_weight)
    result = []
    for other, mine in zip(products[:CHUNKS], products[CHUNKS:]):
        got = lax.ppermute(other, "c", X_PAIRS)
        chip = (mine.astype(jnp.float32) + got.astype(jnp.float32)).reshape(2, PIECE // 4, -1)
        keep = lax.dynamic_index_in_dim(chip, w, 0, keepdims=False)
        give = lax.dynamic_index_in_dim(chip, 1 - w, 0, keepdims=False).astype(jnp.bfloat16)
        landed = lax.ppermute(give, ("x", "w"), pairs(4, lambda i: i ^ 3))
        result.append((keep + landed.astype(jnp.float32)).astype(jnp.bfloat16))
    return jnp.concatenate(result, axis=1)


def solution(mesh):
    inner = Mesh(mesh.devices.reshape(NX, NY, NZ, 2, 2), ("x", "y", "z", "w", "c"))
    ctx, head = ("x", "y", "z"), ("w", "c")
    return jax.shard_map(
        on_device,
        mesh=inner,
        in_specs=(P(ctx, head), P(ctx, head), P(ctx, head), P(ctx), P(), P(), P(head, None)),
        out_specs=P(ctx + head, None),
        check_vma=False,
    )
```

```python
import functools

import jax
import jax.numpy as jnp
import numpy as np
from jax import lax
from jax.experimental import pallas as pl
from jax.experimental.pallas import tpu as pltpu
from jax.sharding import Mesh
from jax.sharding import PartitionSpec as P

EPSILON = 1e-06
HD = 128
PIECE = 128
NX, NY, NZ = 2, 4, 8
GROUP = NX * NY
QUERY_FACTOR = float(168.0**-0.5 / np.log(2.0))
NEGATIVE = -1e30
FREQUENCY = (1000000.0 ** (-2.0 * np.arange(64, dtype=np.float64) / 128)).astype(np.float32)
VMEM_LIMIT = 16 * 1024 * 1024
SMALL = pltpu.CompilerParams(vmem_limit_bytes=8 * 1024 * 1024)
NT = (((1,), (1,)), ((), ()))


def pairs(count, partner):
    return [(i, partner(i)) for i in range(count)]


def z_partner(which, z):
    return z ^ 1 if which == 0 else (((z + 1) ^ 1) + 7) & 7


def y_partner(which, y):
    return y ^ (1, 3)[which]


def by_core(count, partner):
    return tuple(
        [(i * 2 + core, partner(core ^ turn, i) * 2 + core) for i in range(count) for core in range(2)] for turn in range(2)
    )


Z_PAIRS = by_core(NZ, z_partner)
Y_PAIRS = by_core(NY, y_partner)
X_PAIRS = pairs(NX, lambda i: i ^ 1)
BLOCK = 64
STATS = 16
VMEM = pl.BlockSpec(memory_space=pltpu.VMEM)
SMEM = pl.BlockSpec(memory_space=pltpu.SMEM)


def rotate(vector, gain, cosines, sines):
    vector = vector.astype(jnp.float32)
    normed = vector * lax.rsqrt(jnp.mean(vector * vector, axis=-1, keepdims=True) + EPSILON) * gain
    return normed * cosines + pltpu.roll(normed, HD // 2, 1) * sines


def prepare_kernel(q_ref, k_ref, v_ref, pos_ref, freq_ref, q_gain, k_gain, q_out, kv_out):
    lane = lax.broadcasted_iota(jnp.int32, (PIECE, HD), 1)
    spread = jnp.transpose(jnp.broadcast_to(pos_ref[...].astype(jnp.float32), (PIECE, HD)))
    left = lane[:BLOCK] < HD // 2
    angles = jnp.where(left, spread[:BLOCK], spread[BLOCK:]) * freq_ref[...]

    def unpack(packed):
        turned = pltpu.roll(packed, HD // 2, 1)
        return jnp.concatenate([jnp.where(left, packed, turned), jnp.where(left, turned, packed)], axis=0)

    cosines = unpack(jnp.cos(angles))
    sines = jnp.where(lane < HD // 2, -1.0, 1.0) * unpack(jnp.sin(angles))
    for head in range(4):
        cols = slice(head * HD, (head + 1) * HD)
        rows = rotate(q_ref[:, cols], q_gain[...], cosines, sines)
        q_out[:, cols] = (rows * QUERY_FACTOR).astype(jnp.bfloat16)
    for head in range(2):
        cols = slice(head * HD, (head + 1) * HD)
        rows = rotate(k_ref[:, cols], k_gain[...], cosines, sines)
        kv_out[:, cols] = rows.astype(jnp.bfloat16)
    kv_out[:, 2 * HD :] = v_ref[...]


def prepare(queries, keys, values, positions, query_gain, key_gain):
    freq = jnp.asarray(np.concatenate([FREQUENCY, FREQUENCY])[None, :])
    piece = jax.ShapeDtypeStruct((PIECE, 4 * HD), jnp.bfloat16)
    return pl.pallas_call(
        prepare_kernel,
        out_shape=(piece, piece),
        in_specs=[VMEM] * 7,
        out_specs=(VMEM,) * 2,
    )(queries, keys, values, positions[None, :], freq, query_gain[None, :], key_gain[None, :])


def gather_z(own):
    here, there = Z_PAIRS
    one = lax.ppermute(own, ("z", "c"), here)
    two = lax.ppermute(jnp.concatenate([own, one], axis=0), ("z", "c"), there)
    three = lax.ppermute(two, ("z", "c"), here)
    four = lax.ppermute(three, ("z", "c"), there)
    return [own, one, two, three, four]


def z_order(core, z):
    def step(which, place):
        return jnp.where(which == 0, z_partner(0, place), z_partner(1, place))

    def here(place):
        return step(core, place)

    def there(place):
        return step(1 - core, place)

    far, near = there(z), here(z)
    two = [far, here(far)]
    three = [there(near), here(there(near))]
    four = [there(here(far)), here(there(here(far)))]
    return [z, near] + two + three + four


def move_pairs():
    return [(x * NZ + z, x * NZ + ((((z & 3) ^ (3 * x)) << 1) | (z >> 2))) for x in range(NX) for z in range(NZ)]


def gather_xy(own):
    both = jnp.concatenate([own, lax.ppermute(own, "x", X_PAIRS)], axis=0)
    near = lax.ppermute(both, ("y", "c"), Y_PAIRS[0])
    far = lax.ppermute(jnp.concatenate([both, near], axis=0), ("y", "c"), Y_PAIRS[1])
    return both, near, far


def exchange(partial):
    return [
        lax.ppermute(partial[step], ("x", "y"), pairs(GROUP, lambda i: i ^ step)) for step in range(1, GROUP)
    ]


def attention_kernel(ids_ref, *refs):
    own, near, far = refs[:3]
    pieces = refs[3:8]
    out_ref, q_s, k_s, v_s, level_s = refs[8:]
    group, z, core, w = ids_ref[0], ids_ref[1], ids_ref[2], ids_ref[3]
    x, y = group >> 2, group & 3
    first = 1 + 2 * core
    for rel_y, ref, base in ((0, own, 0), (first, near, 0), (4 - first, far, 0), (2, far, 2 * PIECE)):
        for rel_x in range(NX):
            rows = slice(base + rel_x * PIECE, base + (rel_x + 1) * PIECE)
            place = (x ^ rel_x) * NY + (y ^ rel_y)
            for head in range(4):
                q_s[head // 2, place, head % 2] = ref[rows, head * HD : (head + 1) * HD]
    places = z_order(core, z)
    index = 0
    for piece in pieces:
        for part in range(piece.shape[0] // PIECE):
            start = pl.multiple_of(places[index] * PIECE, PIECE)
            rows = slice(part * PIECE, (part + 1) * PIECE)
            for half in range(2):
                k_s[half, pl.ds(start, PIECE), :] = piece[rows, half * HD : (half + 1) * HD]
                v_s[half, pl.ds(start, PIECE), :] = piece[rows, (2 + half) * HD : (3 + half) * HD]
            index += 1
    level_s[...] = jnp.full((PIECE, HD), NEGATIVE, jnp.float32)

    keys = NZ * PIECE
    width = 4 * PIECE

    def slot(source):
        upper = source >> 2
        end_x = ((source >> 1) & 1) ^ w
        end_y = (((source & 1) ^ upper) << 1) | ((z & 1) ^ upper)
        return group ^ ((end_x << 2) | end_y)

    def score(half, pair, masked):
        query = q_s[half, pl.ds(pair * 2, 2)].reshape(width, HD)
        scores = lax.dot_general(query, k_s[half], NT, preferred_element_type=jnp.float32)
        if masked:
            row = lax.broadcasted_iota(jnp.int32, (width, 1), 0)
            source = pair * 2 + row // (2 * PIECE)
            at_z = ((z & 1) << 2) | ((z >> 1) ^ (3 * (source >> 2)))
            last = (source * NZ + at_z) * PIECE + row % PIECE - group * keys
            column = lax.broadcasted_iota(jnp.int32, (width, keys), 1)
            scores = jnp.where(column <= last, scores, NEGATIVE)
        return scores

    def finish(half, pair, scores):
        highest = jnp.max(scores, axis=1, keepdims=True)
        weights = jnp.exp2(scores - highest)
        total = jnp.sum(weights, axis=1, keepdims=True)
        summed = jnp.dot(weights.astype(jnp.bfloat16), v_s[half], preferred_element_type=jnp.float32)
        normal = (summed / total).astype(jnp.bfloat16)
        level = highest + jnp.log2(total)
        lane = lax.broadcasted_iota(jnp.int32, (PIECE, HD), 1)
        for r in range(2):
            step = slot(pair * 2 + r)
            for j in range(2):
                base = (r * 2 + j) * PIECE
                head = half * 2 + j
                out_ref[step, :PIECE, head * HD : (head + 1) * HD] = normal[base : base + PIECE]
                level_s[...] = jnp.where(lane == step * 4 + head, level[base : base + PIECE], level_s[...])

    def run(tiles):
        scores = score(*tiles[0])
        for index, tile in enumerate(tiles):
            following = score(*tiles[index + 1]) if index + 1 < len(tiles) else None
            finish(tile[0], tile[1], scores)
            scores = following

    def body(pair, carry):
        full = pair * 2 > group
        none = pair * 2 + 1 < group

        @pl.when(full)
        def _():
            run([(0, pair, False), (1, pair, False)])

        @pl.when(jnp.logical_not(jnp.logical_or(full, none)))
        def _():
            run([(0, pair, True), (1, pair, True)])

        @pl.when(none)
        def _():
            for r in range(2):
                out_ref[slot(pair * 2 + r), :PIECE, :] = jnp.zeros((PIECE, 4 * HD), jnp.bfloat16)

        return carry

    @pl.when(group < 2)
    def _():
        run([(half, pair, pair == 0) for pair in range(GROUP // 2) for half in range(2)])

    @pl.when(group >= 2)
    def _():
        lax.fori_loop(0, GROUP // 2, body, 0)

    levels = jnp.transpose(level_s[...])
    row = lax.broadcasted_iota(jnp.int32, (STATS, PIECE), 0)
    for step in range(GROUP):
        for head in range(4):
            line = jnp.broadcast_to(levels[step * 4 + head : step * 4 + head + 1], (STATS, PIECE))
            top = line.astype(jnp.bfloat16).astype(jnp.float32)
            middle = (line - top).astype(jnp.bfloat16).astype(jnp.float32)
            rest = line - top - middle
            stats = jnp.where(row == 0, top, jnp.where(row == 1, middle, jnp.where(row == 2, rest, 0.0)))
            out_ref[step, PIECE:, head * HD : (head + 1) * HD] = stats.astype(jnp.bfloat16)


def attention(ids, queries, pieces):
    flops = 2 * 2 * 4 * GROUP * PIECE * NZ * PIECE * HD
    return pl.pallas_call(
        attention_kernel,
        out_shape=jax.ShapeDtypeStruct((GROUP, PIECE + STATS, 4 * HD), jnp.bfloat16),
        in_specs=[SMEM] + [VMEM] * 8,
        out_specs=VMEM,
        scratch_shapes=[
            pltpu.VMEM((2, GROUP, 2, PIECE, HD), jnp.bfloat16),
            pltpu.VMEM((2, NZ * PIECE, HD), jnp.bfloat16),
            pltpu.VMEM((2, NZ * PIECE, HD), jnp.bfloat16),
            pltpu.VMEM((PIECE, HD), jnp.float32),
        ],
        compiler_params=pltpu.CompilerParams(vmem_limit_bytes=36 * 1024 * 1024),
        cost_estimate=pl.CostEstimate(flops=flops, bytes_accessed=2**22, transcendentals=2**22),
    )(ids, *queries, *pieces)


def combine_kernel(ids_ref, partial, *refs):
    pieces = [partial.at[0]] + list(refs[: GROUP - 1])
    keep_out, give_out = refs[GROUP - 1 :]
    second_stays = (ids_ref[0] & 1) == 1
    stats = [piece[PIECE:, :].astype(jnp.float32) for piece in pieces]
    levels = [s[0:1] + s[1:2] + s[2:3] for s in stats]
    highest = functools.reduce(jnp.maximum, levels)
    shares = [jnp.exp2(level - highest) for level in levels]
    scale = 1.0 / functools.reduce(jnp.add, shares)
    table = jnp.concatenate([share * scale for share in shares], axis=0)
    for head in range(4):
        lanes = slice(head * HD, (head + 1) * HD)
        columns = jnp.transpose(table[:, lanes])
        totals = []
        for first in (0, BLOCK):
            rows = slice(first, first + BLOCK)
            total = None
            for s in range(GROUP):
                term = pieces[s][rows, lanes].astype(jnp.float32) * columns[rows, s : s + 1]
                total = term if total is None else total + term
            totals.append(total)
        keep_out[:, lanes] = jnp.where(second_stays, totals[1], totals[0]).astype(jnp.bfloat16)
        give_out[:, lanes] = jnp.where(second_stays, totals[0], totals[1]).astype(jnp.bfloat16)


def combine(ids, partial, received):
    block = jax.ShapeDtypeStruct((BLOCK, 4 * HD), jnp.bfloat16)
    return pl.pallas_call(
        combine_kernel,
        out_shape=(block, block),
        in_specs=[SMEM] + [VMEM] * GROUP,
        out_specs=(VMEM, VMEM),
        compiler_params=SMALL,
    )(ids, partial, *received)


TILE = 896


CHUNKS = 3


def project_kernel(ids_ref, kept, taken, weight, *refs):
    others, mines, rows_s = refs[:CHUNKS], refs[CHUNKS : 2 * CHUNKS], refs[-1]
    core = ids_ref[2]
    quarter = PIECE // 4
    kept_high = ((ids_ref[0] ^ ids_ref[1]) & 1) == 1
    first, second = kept[...], taken[...]
    low = jnp.where(kept_high, second, first)
    high = jnp.where(kept_high, first, second)
    for k, block in enumerate((low, high)):
        for part in range(2):
            own = 1 - (part ^ core)
            start = pl.multiple_of(own * BLOCK + k * quarter, quarter)
            rows_s[pl.ds(start, quarter), :] = block[part * quarter : (part + 1) * quarter]
    rows = rows_s[...]
    tiles = weight.shape[1] // CHUNKS // TILE
    for chunk in range(CHUNKS):
        for tile in range(tiles):
            lanes = slice(tile * TILE, (tile + 1) * TILE)
            start = (chunk * tiles + tile) * TILE
            product = jnp.dot(rows, weight[:, start : start + TILE], preferred_element_type=jnp.float32)
            product = product.astype(jnp.bfloat16)
            others[chunk][:, lanes] = product[:BLOCK]
            mines[chunk][:, lanes] = product[BLOCK:]


def project(ids, kept, taken, out_weight):
    half = jax.ShapeDtypeStruct((BLOCK, out_weight.shape[1] // CHUNKS), jnp.bfloat16)
    return pl.pallas_call(
        project_kernel,
        out_shape=(half,) * (2 * CHUNKS),
        in_specs=[SMEM] + [VMEM] * 3,
        out_specs=(VMEM,) * (2 * CHUNKS),
        scratch_shapes=[pltpu.VMEM((PIECE, 4 * HD), jnp.bfloat16)],
        compiler_params=pltpu.CompilerParams(vmem_limit_bytes=VMEM_LIMIT),
        cost_estimate=pl.CostEstimate(flops=2 * PIECE * 512 * 5376, bytes_accessed=2**23, transcendentals=0),
    )(ids, kept, taken, out_weight)


def on_device(queries, keys, values, positions, query_gain, key_gain, out_weight):
    x, y, z = lax.axis_index("x"), lax.axis_index("y"), lax.axis_index("z")
    w, c = lax.axis_index("w"), lax.axis_index("c")
    ids = jnp.stack([x * NY + y, z, c, w]).astype(jnp.int32)
    query_rows, key_rows = prepare(queries, keys, values, positions, query_gain, key_gain)
    moved = lax.ppermute(query_rows, ("x", "z"), move_pairs())
    pieces = gather_z(key_rows)
    partial = attention(ids, gather_xy(moved), pieces)
    kept, given = combine(ids, partial, exchange(partial))
    taken = lax.ppermute(given, "z", pairs(NZ, lambda i: i ^ 1))
    products = project(ids, kept, taken, out_weight)
    result = []
    for other, mine in zip(products[:CHUNKS], products[CHUNKS:]):
        got = lax.ppermute(other, "c", X_PAIRS)
        chip = (mine.astype(jnp.float32) + got.astype(jnp.float32)).reshape(2, PIECE // 4, -1)
        keep = lax.dynamic_index_in_dim(chip, w, 0, keepdims=False)
        give = lax.dynamic_index_in_dim(chip, 1 - w, 0, keepdims=False).astype(jnp.bfloat16)
        landed = lax.ppermute(give, ("x", "w"), pairs(4, lambda i: i ^ 3))
        result.append((keep + landed.astype(jnp.float32)).astype(jnp.bfloat16))
    return jnp.concatenate(result, axis=1)


def solution(mesh):
    inner = Mesh(mesh.devices.reshape(NX, NY, NZ, 2, 2), ("x", "y", "z", "w", "c"))
    ctx, head = ("x", "y", "z"), ("w", "c")
    return jax.shard_map(
        on_device,
        mesh=inner,
        in_specs=(P(ctx, head), P(ctx, head), P(ctx, head), P(ctx), P(), P(), P(head, None)),
        out_specs=P(ctx + head, None),
        check_vma=False,
    )
```
